32 devices in a mesh: blk: 16 (over z, y, core), cset: 2 (over x).
Axes of the slice: x: 2, y: 2, z: 4, core: 2. Of those that a mesh axis runs over, the one named last changes fastest.
Arguments:
- active_table: bfloat16 [8192, 256], P(('blk', 'cset')), may hold values from 0.019897461 to 0.19921875
- passive_table: bfloat16 [8192, 256], P(('blk', 'cset')), may hold values from 0 to 0.15
- adjacency: bfloat16 [16, 2, 5, 8, 128, 128], P('blk', 'cset'), may hold values from 0 to 1, as said below
- tile_dst: int32 [16, 2, 5, 8], P('blk', 'cset'), may hold values from 0 to 1
- tile_src: int32 [16, 2, 5, 8], P('blk', 'cset'), may hold values from 0 to 3
- tile_count: int32 [16, 2, 5], P('blk', 'cset'), may hold values from 1 to 8, as said below
- split_active: int32 [20, 924], replicated, may hold values from 0 to 219, as said below
- split_passive: int32 [20, 924], replicated, may hold values from 0 to 219, as said below
Outputs:
- joined_table: bfloat16 [8192, 1024], P('blk', 'cset')
The draws below stay inside these ranges and needn't reach their ends.
Inputs may be any that keep to these rules, and one draw needn't show every extreme that they name: For each six-color set s, the 20 pairs (split_active[j, s], split_passive[j, s]) name its 20 divisions into an ordered pair of three-color sets, each once, as columns of the two child tables; a child table's columns hold its 220 color sets in some fixed order, and columns 220 and above are never named. `split_passive`: see split_active; each table is a column order of its own. `tile_count`: the own partition's slot r = 2 is full on every device. `adjacency`: edge weights are 0 or 1.
All inputs are finite; a program needn't handle non-finite values.
Results may differ from the reference program's by a relative error of at most 0.0026.
Values may be sent and summed in bfloat16 or wider, within the bound.
A program may use at most 64 MiB of HBM per device.

```python
import math
import jax
import jax.numpy as jnp
import numpy as np
from jax import lax

K = 12
CHILD = 220
OUT = 924
CPAD = 256
OUTPAD = 1024
TILE = 128
TPP = 8
RDEV = 256
REACH_HALF = 2
REACH = 5
PR = 512
V = 8192
N_BLK = 16
N_CSET = 2


def count_members(candidate):
    total = 0
    for position in range(K):
        total = total + (candidate >> position & 1)
    return total


def subset_tables():

    def subsets_of(members):
        return [candidate for candidate in range(1 << K) if count_members(candidate) == members]
    smaller = subsets_of(3)
    ranking = {}
    for position, candidate in enumerate(smaller):
        ranking[candidate] = position
    leading = []
    trailing = []
    for parent in subsets_of(6):
        inside = [candidate for candidate in smaller if candidate & parent == candidate]
        leading.append([ranking[candidate] for candidate in inside])
        trailing.append([ranking[parent ^ candidate] for candidate in inside])
    return (np.array(leading, dtype=np.int32).T, np.array(trailing, dtype=np.int32).T)


def row_counts(key, low, high, factor_low, factor_high):
    key_scale, key_factor, key_keep = jax.random.split(key, 3)
    exponent = jax.random.uniform(key_scale, (V, 1), jnp.float32, math.log(low), math.log(high))
    factor = jax.random.uniform(key_factor, (V, CPAD), jnp.float32, factor_low, factor_high)
    keep = jax.random.bernoulli(key_keep, 0.5, (V, CPAD)).astype(jnp.float32)
    return jnp.exp(exponent) * factor * keep


def draw_passive_table(key, part):
    key = jax.random.fold_in(key, 5)
    values = row_counts(key, 0.0001, 0.1, 0.5, 1.5)
    return values.astype(jnp.bfloat16)


def draw_adjacency(key, part):
    key = jax.random.fold_in(key, 1)
    key_density, key_edges = jax.random.split(key)
    shape = (N_BLK, N_CSET, REACH, TPP, TILE, TILE)
    level = jax.random.uniform(key_density, (N_BLK, N_CSET, REACH, TPP, 1, 1), jnp.float32, math.log(0.01), math.log(0.3))
    density = jnp.exp(level)
    edges = jax.random.bernoulli(key_edges, density, shape)
    return edges.astype(jnp.float32).astype(jnp.bfloat16)


def draw_tile_count(key, part):
    key = jax.random.fold_in(key, 2)
    counts = jax.random.randint(key, (N_BLK, N_CSET, REACH), 1, TPP + 1, dtype=jnp.int32)
    return counts.at[:, :, REACH_HALF].set(TPP)


def draw_split_active(key, part):
    key = jax.random.fold_in(key, 3)
    leading, trailing = subset_tables()
    order = jax.random.permutation(key, CHILD).astype(jnp.int32)
    return order[jnp.asarray(leading)]


def draw_split_passive(key, part):
    key = jax.random.fold_in(key, 4)
    leading, trailing = subset_tables()
    order = jax.random.permutation(key, CHILD).astype(jnp.int32)
    return order[jnp.asarray(trailing)]


def touch_ends(result, own_key, least, high):
    spot = [jax.random.randint(jax.random.fold_in(own_key, axis), (), 0, length) for axis, length in enumerate(result.shape)]
    main_axis = result.shape.index(max(result.shape))
    next_to = spot[:main_axis] + [(spot[main_axis] + 1) % result.shape[main_axis]] + spot[main_axis + 1:]
    return result.at[tuple(spot)].set(least).at[tuple(next_to)].set(high)


def block_levels(rng, extent, shards, smallest, high):
    loudness = 1.0
    for dim, blocks in shards:
        draws = jax.random.uniform(jax.random.fold_in(jax.random.fold_in(rng, 6), dim), (blocks,), jnp.float32, smallest / len(shards), high / len(shards))
        loudness = loudness * jnp.repeat(jnp.exp(draws), extent[dim] // blocks).reshape((-1,) + (1,) * (len(extent) - 1 - dim))
    return loudness


def setup_inputs(seed: int = 0) -> dict:
    keys = jax.random.split(jax.random.key(seed), 9)
    return {
        "active_table": jnp.clip(jnp.exp(math.log(0.19921875) - 2.3038113 * jax.random.uniform(keys[0], (V, CPAD), jnp.float32) ** block_levels(keys[0], (V, CPAD), ((0, 32),), -0.2, 0.2)), 0.019897461, 0.19921875).astype(jnp.bfloat16),
        "passive_table": draw_passive_table(jax.random.fold_in(keys[8], 71), 0),
        "adjacency": draw_adjacency(jax.random.fold_in(keys[8], 71), 0),
        "tile_dst": touch_ends(jax.random.randint(keys[3], (N_BLK, N_CSET, REACH, TPP), 0, RDEV // TILE), jax.random.fold_in(keys[3], 1), 0, (RDEV // TILE) - 1).astype(jnp.int32),
        "tile_src": touch_ends(jax.random.randint(keys[4], (N_BLK, N_CSET, REACH, TPP), 0, RDEV * N_CSET // TILE), jax.random.fold_in(keys[4], 1), 0, (RDEV * N_CSET // TILE) - 1).astype(jnp.int32),
        "tile_count": draw_tile_count(jax.random.fold_in(keys[8], 71), 0),
        "split_active": draw_split_active(jax.random.fold_in(keys[8], 71), 0),
        "split_passive": draw_split_passive(jax.random.fold_in(keys[8], 71), 0),
    }


def reference(active_table, passive_table, adjacency, tile_dst, tile_src, tile_count, split_active, split_passive):
    device_count = N_BLK * N_CSET
    source_blocks = passive_table.reshape(N_BLK, PR // TILE, TILE, CPAD)
    tiles_flat = adjacency.reshape(device_count, REACH, TPP, TILE, TILE)
    dst_flat = tile_dst.reshape(device_count, REACH, TPP)
    src_flat = tile_src.reshape(device_count, REACH, TPP)
    count_flat = tile_count.reshape(device_count, REACH)
    slot_ids = jnp.arange(TPP, dtype=jnp.int32)
    reach_ids = jnp.arange(REACH, dtype=jnp.int32)
    row_tiles = jnp.arange(RDEV // TILE, dtype=jnp.int32)

    def one_device(device):
        block_index = device // N_CSET
        partitions = (block_index + reach_ids - REACH_HALF) % N_BLK
        chosen = source_blocks[partitions[:, None], src_flat[device]].astype(jnp.float32)
        live = (slot_ids[None, :] < count_flat[device][:, None]).astype(jnp.float32)
        weights = tiles_flat[device].astype(jnp.float32) * live[:, :, None, None]
        product = jnp.einsum('rtij,rtjc->rtic', weights, chosen, precision=lax.Precision.HIGHEST)
        placing = (dst_flat[device][:, :, None] == row_tiles[None, None, :]).astype(jnp.float32)
        summed = jnp.einsum('rtd,rtic->dic', placing, product, precision=lax.Precision.HIGHEST)
        return summed.reshape(RDEV, CPAD)

    neighbour = lax.map(one_device, jnp.arange(device_count, dtype=jnp.int32))
    neighbour = neighbour.reshape(V, CPAD).astype(jnp.bfloat16)

    def one_partition(index):
        start = index * PR
        left = lax.dynamic_slice_in_dim(active_table, start, PR, 0)
        right = lax.dynamic_slice_in_dim(neighbour, start, PR, 0)
        picked_left = jnp.take(left, split_active, axis=1).astype(jnp.float32)
        picked_right = jnp.take(right, split_passive, axis=1).astype(jnp.float32)
        joined = jnp.sum(picked_left * picked_right, axis=1).astype(jnp.bfloat16)
        return jnp.pad(joined, ((0, 0), (0, OUTPAD - OUT)))

    joined_table = lax.map(one_partition, jnp.arange(N_BLK, dtype=jnp.int32))
    return joined_table.reshape(V, OUTPAD)
```

```python
import functools

import jax
import jax.numpy as jnp
from jax import lax
from jax.experimental import pallas as pl
from jax.experimental.pallas import tpu as pltpu
from jax.sharding import PartitionSpec as P

OUTPAD = 1024
TILE = 128
MESH = pl.DeviceIdType.MESH


def kernel(
    n_blk,
    n_cset,
    half,
    dst_s,
    src_s,
    count_s,
    active_h,
    passive_h,
    adjacency_h,
    left_h,
    right_h,
    out_h,
    active_v,
    left_raw,
    right_raw,
    left_v,
    right_v,
    tiles_v,
    dense_v,
    picked_v,
    choose_v,
    neighbour_v,
    result_v,
    *rest,
):
    home = rest[: half + 1]
    away = (None,) + rest[half + 1 : 2 * half + 1]
    (
        local_sem,
        own_send,
        side_send,
        sibling_send,
        home_recv,
        away_recv,
        out_send,
        out_recv,
        out_local,
    ) = rest[2 * half + 1 :]
    b = lax.axis_index("blk")
    c = lax.axis_index("cset")
    rows, channels = active_v.shape
    splits, sets = left_raw.shape
    width = out_h.shape[1]
    piece = min(width, 256)
    sign = 2 * (b % 2) - 1
    sibling = (b - sign, c)
    others = [(c + i) % n_cset for i in range(1, n_cset)]
    targets = [None] + [
        ((b + k * (1 - 2 * ((b - k + n_blk) % 2)) + n_blk) % n_blk, c) for k in range(1, half + 1)
    ]
    sources = [None] + [((b + sign * k + n_blk) % n_blk, c) for k in range(1, half + 1)]

    barrier = pltpu.get_barrier_semaphore()
    senders = sources[1:] + [sibling] + [(b, o) for o in others]
    for device in senders:
        pl.semaphore_signal(barrier, inc=1, device_id=device, device_id_type=MESH)

    mine = pl.ds(pl.multiple_of(c * rows, rows), rows)
    copies = [
        pltpu.make_async_copy(left_h, left_raw, local_sem.at[0]),
        pltpu.make_async_copy(right_h, right_raw, local_sem.at[1]),
        pltpu.make_async_copy(active_h, active_v, local_sem.at[2]),
        pltpu.make_async_copy(adjacency_h, tiles_v, local_sem.at[3]),
        pltpu.make_async_copy(passive_h, home[0].at[mine, :], local_sem.at[4]),
    ]
    for copy in copies:
        copy.start()
    pl.semaphore_wait(barrier, len(senders))

    started = []

    def part(cset):
        return pl.ds(pl.multiple_of(cset * rows, rows), rows)

    def send(src, dst, send_sem, recv_sem, device):
        copy = pltpu.make_async_remote_copy(
            src_ref=src,
            dst_ref=dst,
            send_sem=send_sem,
            recv_sem=recv_sem,
            device_id=device,
            device_id_type=MESH,
        )
        copy.start()
        started.append(copy)

    def to_others(block, k):
        for i, other in enumerate(others):
            send(block, home[k].at[mine, :], side_send.at[k, i], home_recv.at[k, c], (b, other))

    def to_sibling(block, k, cset):
        send(
            block,
            away[k + 1].at[part(cset), :],
            sibling_send.at[k, cset],
            away_recv.at[k, cset],
            sibling,
        )

    def arrived(ref, cset, sem):
        pltpu.make_async_copy(ref.at[part(cset), :], ref.at[part(cset), :], sem).wait()

    for k in range(half, 0, -1):
        send(passive_h, home[k].at[mine, :], own_send.at[k], home_recv.at[k, c], targets[k])
    to_others(passive_h, 0)
    to_sibling(passive_h, 0, c)

    copies[0].wait()
    copies[1].wait()
    left_v[...] = jnp.full(left_v.shape, -1, jnp.int32)
    right_v[...] = jnp.full(right_v.shape, -1, jnp.int32)
    left_v[:splits, :sets] = left_raw[...]
    right_v[:splits, :sets] = right_raw[...]
    copies[2].wait()
    copies[3].wait()

    def assemble(r, carry):
        for d in range(rows // TILE):
            for e in range(n_cset * rows // TILE):
                total = jnp.zeros((TILE, TILE), jnp.bfloat16)
                for t in range(tiles_v.shape[1]):
                    here = (dst_s[r, t] == d) & (src_s[r, t] == e) & (count_s[r] > t)
                    total = total + jnp.where(here, tiles_v[r, t], jnp.zeros_like(total))
                dense_v[r, d * TILE : (d + 1) * TILE, e * TILE : (e + 1) * TILE] = total
        return carry

    channel = lax.broadcasted_iota(jnp.int32, (channels, 256), 0)

    def pick(j, carry):
        for at in range(0, OUTPAD, 256):
            columns = slice(at, at + 256)
            left_one = (left_v[pl.ds(j, 1), columns] == channel).astype(jnp.bfloat16)
            right_one = (right_v[pl.ds(j, 1), columns] == channel).astype(jnp.bfloat16)
            choose_v[j, :, columns] = right_one
            picked = jnp.dot(active_v[...], left_one, preferred_element_type=jnp.float32)
            picked_v[j, :, columns] = picked.astype(jnp.bfloat16)
        return carry

    def side_arrived(k):
        for other in others:
            arrived(home[k], other, home_recv.at[k, other])
            if k < half:
                to_sibling(home[k].at[part(other), :], k, other)

    def own_arrived(k):
        arrived(home[k], c, home_recv.at[k, c])
        to_others(home[k].at[mine, :], k)
        if k < half:
            to_sibling(home[k].at[mine, :], k, c)

    stages = [functools.partial(own_arrived, 1), functools.partial(side_arrived, 0)]
    for k in range(2, half + 1):
        stages += [functools.partial(own_arrived, k), functools.partial(side_arrived, k - 1)]

    lax.fori_loop(0, 2 * half + 1, assemble, 0)
    for i, stage in enumerate(stages):
        lax.fori_loop(splits * i // len(stages), splits * (i + 1) // len(stages), pick, 0)
        stage()

    def times(r, ref):
        return jnp.dot(dense_v[r], ref[...], preferred_element_type=jnp.float32)

    copies[4].wait()
    total = times(half, home[0])
    for k in range(1, half):
        total = total + times(half + sign * k, home[k])
    for k in range(1, half + 1):
        for cset in [c] + others:
            arrived(away[k], cset, away_recv.at[k - 1, cset])
        total = total + times(half - sign * k, away[k])
    side_arrived(half)
    total = total + times(half + sign * half, home[half])
    neighbour_v[...] = total.astype(jnp.bfloat16)

    results = []
    for i, owner in enumerate(others + [c]):
        for p in range(width // piece):
            columns = pl.ds(pl.multiple_of(owner * width + p * piece, piece), piece)

            def step(g, total):
                for u in range(4):
                    j = g * 4 + u
                    found = jnp.dot(
                        neighbour_v[...],
                        choose_v[j, :, columns],
                        preferred_element_type=jnp.float32,
                    )
                    total = total + picked_v[j, :, columns].astype(jnp.float32) * found
                return total

            total = lax.fori_loop(0, splits // 4, step, jnp.zeros((rows, piece), jnp.float32))
            result_v[i, :, p * piece : (p + 1) * piece] = total.astype(jnp.bfloat16)
            block = result_v.at[i, :, pl.ds(p * piece, piece)]
            goal = out_h.at[mine, pl.ds(p * piece, piece)]
            if i < n_cset - 1:
                send(block, goal, out_send.at[i, p], out_recv.at[c, p], (b, owner))
            else:
                copy = pltpu.make_async_copy(block, goal, out_local.at[p])
                copy.start()
                results.append(copy)
    for copy in results:
        copy.wait()
    for copy in started:
        copy.wait_send()
    for other in others:
        for p in range(width // piece):
            block = out_h.at[part(other), pl.ds(p * piece, piece)]
            pltpu.make_async_copy(block, block, out_recv.at[other, p]).wait()


def local(
    active_table,
    passive_table,
    adjacency,
    tile_dst,
    tile_src,
    tile_count,
    split_active,
    split_passive,
):
    n_blk, n_cset = lax.axis_size("blk"), lax.axis_size("cset")
    rows, channels = passive_table.shape
    tiles = adjacency[0, 0]
    reach, slots = tiles.shape[:2]
    half = (reach - 1) // 2
    splits, sets = split_active.shape
    width = OUTPAD // n_cset
    pieces = width // min(width, 256)
    hbm = pl.BlockSpec(memory_space=pl.ANY)
    smem = pl.BlockSpec(memory_space=pltpu.SMEM)
    bf16 = jnp.bfloat16
    dma = pltpu.SemaphoreType.DMA
    table = (-(-splits // 8) * 8, OUTPAD)
    return pl.pallas_call(
        functools.partial(kernel, n_blk, n_cset, half),
        out_shape=jax.ShapeDtypeStruct((n_cset * rows, width), bf16),
        in_specs=[smem] * 3 + [hbm] * 5,
        out_specs=hbm,
        scratch_shapes=[
            pltpu.VMEM((rows, channels), bf16),
            pltpu.VMEM((splits, sets), jnp.int32),
            pltpu.VMEM((splits, sets), jnp.int32),
            pltpu.VMEM(table, jnp.int32),
            pltpu.VMEM(table, jnp.int32),
            pltpu.VMEM((reach, slots, TILE, TILE), bf16),
            pltpu.VMEM((reach, rows, n_cset * rows), bf16),
            pltpu.VMEM((splits, rows, OUTPAD), bf16),
            pltpu.VMEM((splits, channels, OUTPAD), bf16),
            pltpu.VMEM((rows, channels), bf16),
            pltpu.VMEM((n_cset, rows, width), bf16),
        ]
        + [pltpu.VMEM((n_cset * rows, channels), bf16)] * (2 * half + 1)
        + [
            dma((5,)),
            dma((half + 1,)),
            dma((half + 1, n_cset)),
            dma((half, n_cset)),
            dma((half + 1, n_cset)),
            dma((half, n_cset)),
            dma((n_cset, pieces)),
            dma((n_cset, pieces)),
            dma((pieces,)),
        ],
        compiler_params=pltpu.CompilerParams(
            collective_id=0, has_side_effects=True, vmem_limit_bytes=56 * 1024 * 1024
        ),
    )(
        tile_dst[0, 0],
        tile_src[0, 0],
        tile_count[0, 0],
        active_table,
        passive_table,
        tiles,
        split_active,
        split_passive,
    )


def solution(mesh):
    in_specs = (
        P(("blk", "cset"), None),
        P(("blk", "cset"), None),
        P("blk", "cset", None, None, None, None),
        P("blk", "cset", None, None),
        P("blk", "cset", None, None),
        P("blk", "cset", None),
        P(),
        P(),
    )
    out_specs = P("blk", "cset")
    return jax.shard_map(local, mesh=mesh, in_specs=in_specs, out_specs=out_specs, check_vma=False)
```

```python
import functools

import jax
import jax.numpy as jnp
from jax import lax
from jax.experimental import pallas as pl
from jax.experimental.pallas import tpu as pltpu
from jax.sharding import PartitionSpec as P

OUTPAD = 1024
TILE = 128
MESH = pl.DeviceIdType.MESH


def kernel(
    n_blk,
    n_cset,
    half,
    dst_s,
    src_s,
    count_s,
    active_h,
    passive_h,
    adjacency_h,
    left_h,
    right_h,
    out_h,
    active_v,
    left_raw,
    right_raw,
    left_v,
    right_v,
    tiles_v,
    dense_v,
    picked_v,
    choose_v,
    neighbour_v,
    result_v,
    *rest,
):
    home = rest[: half + 1]
    away = (None,) + rest[half + 1 : 2 * half + 1]
    (
        local_sem,
        own_send,
        side_send,
        sibling_send,
        home_recv,
        away_recv,
        out_send,
        out_recv,
        out_local,
    ) = rest[2 * half + 1 :]
    b = lax.axis_index("blk")
    c = lax.axis_index("cset")
    rows, channels = active_v.shape
    splits, sets = left_raw.shape
    width = out_h.shape[1]
    piece = min(width, 256)
    sign = 2 * (b % 2) - 1
    sibling = (b - sign, c)
    others = [(c + i) % n_cset for i in range(1, n_cset)]
    targets = [None] + [
        ((b + k * (1 - 2 * ((b - k + n_blk) % 2)) + n_blk) % n_blk, c) for k in range(1, half + 1)
    ]
    sources = [None] + [((b + sign * k + n_blk) % n_blk, c) for k in range(1, half + 1)]

    barrier = pltpu.get_barrier_semaphore()
    senders = sources[1:] + [sibling] + [(b, o) for o in others]
    for device in senders:
        pl.semaphore_signal(barrier, inc=1, device_id=device, device_id_type=MESH)

    mine = pl.ds(pl.multiple_of(c * rows, rows), rows)
    copies = [
        pltpu.make_async_copy(left_h, left_raw, local_sem.at[0]),
        pltpu.make_async_copy(right_h, right_raw, local_sem.at[1]),
        pltpu.make_async_copy(active_h, active_v, local_sem.at[2]),
        pltpu.make_async_copy(adjacency_h, tiles_v, local_sem.at[3]),
        pltpu.make_async_copy(passive_h, home[0].at[mine, :], local_sem.at[4]),
    ]
    for copy in copies:
        copy.start()
    pl.semaphore_wait(barrier, len(senders))

    started = []

    def part(cset):
        return pl.ds(pl.multiple_of(cset * rows, rows), rows)

    def send(src, dst, send_sem, recv_sem, device):
        copy = pltpu.make_async_remote_copy(
            src_ref=src,
            dst_ref=dst,
            send_sem=send_sem,
            recv_sem=recv_sem,
            device_id=device,
            device_id_type=MESH,
        )
        copy.start()
        started.append(copy)

    def to_others(block, k):
        for i, other in enumerate(others):
            send(block, home[k].at[mine, :], side_send.at[k, i], home_recv.at[k, c], (b, other))

    def to_sibling(block, k, cset):
        send(
            block,
            away[k + 1].at[part(cset), :],
            sibling_send.at[k, cset],
            away_recv.at[k, cset],
            sibling,
        )

    def arrived(ref, cset, sem):
        pltpu.make_async_copy(ref.at[part(cset), :], ref.at[part(cset), :], sem).wait()

    for k in range(half, 0, -1):
        send(passive_h, home[k].at[mine, :], own_send.at[k], home_recv.at[k, c], targets[k])
    to_others(passive_h, 0)
    to_sibling(passive_h, 0, c)

    copies[0].wait()
    copies[1].wait()
    left_v[...] = jnp.full(left_v.shape, -1, jnp.float32)
    right_v[...] = jnp.full(right_v.shape, -1, jnp.float32)
    left_v[:splits, :sets] = left_raw[...].astype(jnp.float32)
    right_v[:splits, :sets] = right_raw[...].astype(jnp.float32)
    copies[2].wait()
    copies[3].wait()

    def assemble(r, carry):
        for d in range(rows // TILE):
            for e in range(n_cset * rows // TILE):
                total = jnp.zeros((TILE, TILE), jnp.bfloat16)
                for t in range(tiles_v.shape[1]):
                    here = (dst_s[0, r, 0, t] == d) & (src_s[0, r, 0, t] == e) & (count_s[0, 0, r] > t)
                    total = total + jnp.where(here, tiles_v[r, t], jnp.zeros_like(total))
                dense_v[r, d * TILE : (d + 1) * TILE, e * TILE : (e + 1) * TILE] = total
        return carry

    channel = lax.broadcasted_iota(jnp.int32, (channels, 256), 0).astype(jnp.bfloat16)
    one, zero = jnp.ones(channel.shape, jnp.bfloat16), jnp.zeros(channel.shape, jnp.bfloat16)

    def one_hot(table, j, columns):
        row = jnp.broadcast_to(table[pl.ds(j, 1), columns], (16, 256)).astype(jnp.bfloat16)
        return jnp.where(jnp.concatenate([row] * (channels // 16), axis=0) == channel, one, zero)

    def pick(j, carry):
        for at in range(0, OUTPAD, 256):
            columns = slice(at, at + 256)
            choose_v[j, :, columns] = one_hot(right_v, j, columns)
            picked = jnp.dot(
                active_v[...], one_hot(left_v, j, columns), preferred_element_type=jnp.float32
            )
            picked_v[j, :, columns] = picked.astype(jnp.bfloat16)
        return carry

    def side_arrived(k):
        for other in others:
            arrived(home[k], other, home_recv.at[k, other])
            if k < half:
                to_sibling(home[k].at[part(other), :], k, other)

    def own_arrived(k):
        arrived(home[k], c, home_recv.at[k, c])
        to_others(home[k].at[mine, :], k)
        if k < half:
            to_sibling(home[k].at[mine, :], k, c)

    stages = [functools.partial(own_arrived, 1), functools.partial(side_arrived, 0)]
    for k in range(2, half + 1):
        stages += [functools.partial(own_arrived, k), functools.partial(side_arrived, k - 1)]

    lax.fori_loop(0, 2 * half + 1, assemble, 0)
    for i, stage in enumerate(stages):
        lax.fori_loop(splits * i // len(stages), splits * (i + 1) // len(stages), pick, 0)
        stage()

    def times(r, ref):
        return jnp.dot(dense_v[r], ref[...], preferred_element_type=jnp.float32)

    copies[4].wait()
    total = times(half, home[0])
    for k in range(1, half):
        total = total + times(half + sign * k, home[k])
    for k in range(1, half + 1):
        for cset in [c] + others:
            arrived(away[k], cset, away_recv.at[k - 1, cset])
        total = total + times(half - sign * k, away[k])
    side_arrived(half)
    total = total + times(half + sign * half, home[half])
    neighbour_v[...] = total.astype(jnp.bfloat16)

    results = []
    for i, owner in enumerate(others + [c]):
        for p in range(width // piece):
            columns = pl.ds(pl.multiple_of(owner * width + p * piece, piece), piece)

            def step(g, total):
                for u in range(4):
                    j = g * 4 + u
                    found = jnp.dot(
                        neighbour_v[...],
                        choose_v[j, :, columns],
                        preferred_element_type=jnp.float32,
                    )
                    total = total + picked_v[j, :, columns].astype(jnp.float32) * found
                return total

            total = lax.fori_loop(0, splits // 4, step, jnp.zeros((rows, piece), jnp.float32))
            result_v[i, :, p * piece : (p + 1) * piece] = total.astype(jnp.bfloat16)
            block = result_v.at[i, :, pl.ds(p * piece, piece)]
            goal = out_h.at[mine, pl.ds(p * piece, piece)]
            if i < n_cset - 1:
                send(block, goal, out_send.at[i, p], out_recv.at[c, p], (b, owner))
            else:
                copy = pltpu.make_async_copy(block, goal, out_local.at[p])
                copy.start()
                results.append(copy)
    for copy in results:
        copy.wait()
    for copy in started:
        copy.wait_send()
    for other in others:
        for p in range(width // piece):
            block = out_h.at[part(other), pl.ds(p * piece, piece)]
            pltpu.make_async_copy(block, block, out_recv.at[other, p]).wait()


def hand_over(joined_h, out_h, sem):
    rows = out_h.shape[0] // 8
    copies = []
    for i in range(8):
        block = pl.ds(i * rows, rows)
        copies.append(pltpu.make_async_copy(joined_h.at[block, :], out_h.at[block, :], sem.at[i]))
        copies[i].start()
    for copy in copies:
        copy.wait()


def local(
    active_table,
    passive_table,
    adjacency,
    tile_dst,
    tile_src,
    tile_count,
    split_active,
    split_passive,
):
    n_blk, n_cset = lax.axis_size("blk"), lax.axis_size("cset")
    rows, channels = passive_table.shape
    tiles = adjacency[0, 0]
    reach, slots = tiles.shape[:2]
    half = (reach - 1) // 2
    splits, sets = split_active.shape
    width = OUTPAD // n_cset
    pieces = width // min(width, 256)
    hbm = pl.BlockSpec(memory_space=pl.ANY)
    smem = pl.BlockSpec(memory_space=pltpu.SMEM)
    bf16 = jnp.bfloat16
    dma = pltpu.SemaphoreType.DMA
    table = (-(-splits // 8) * 8, OUTPAD)
    joined = pl.pallas_call(
        functools.partial(kernel, n_blk, n_cset, half),
        out_shape=jax.ShapeDtypeStruct((n_cset * rows, width), bf16),
        in_specs=[smem] * 3 + [hbm] * 5,
        out_specs=hbm,
        scratch_shapes=[
            pltpu.VMEM((rows, channels), bf16),
            pltpu.VMEM((splits, sets), jnp.int32),
            pltpu.VMEM((splits, sets), jnp.int32),
            pltpu.VMEM(table, jnp.float32),
            pltpu.VMEM(table, jnp.float32),
            pltpu.VMEM((reach, slots, TILE, TILE), bf16),
            pltpu.VMEM((reach, rows, n_cset * rows), bf16),
            pltpu.VMEM((splits, rows, OUTPAD), bf16),
            pltpu.VMEM((splits, channels, OUTPAD), bf16),
            pltpu.VMEM((rows, channels), bf16),
            pltpu.VMEM((n_cset, rows, width), bf16),
        ]
        + [pltpu.VMEM((n_cset * rows, channels), bf16)] * (2 * half + 1)
        + [
            dma((5,)),
            dma((half + 1,)),
            dma((half + 1, n_cset)),
            dma((half, n_cset)),
            dma((half + 1, n_cset)),
            dma((half, n_cset)),
            dma((n_cset, pieces)),
            dma((n_cset, pieces)),
            dma((pieces,)),
        ],
        compiler_params=pltpu.CompilerParams(
            collective_id=0, has_side_effects=True, vmem_limit_bytes=56 * 1024 * 1024
        ),
    )(
        jnp.transpose(tile_dst, (0, 2, 1, 3)),
        jnp.transpose(tile_src, (0, 2, 1, 3)),
        tile_count,
        active_table,
        passive_table,
        tiles,
        split_active,
        split_passive,
    )
    return pl.pallas_call(
        hand_over,
        out_shape=joined,
        in_specs=[hbm],
        out_specs=hbm,
        scratch_shapes=[dma((8,))],
        compiler_params=pltpu.CompilerParams(vmem_limit_bytes=56 * 1024 * 1024),
    )(joined)


def solution(mesh):
    in_specs = (
        P(("blk", "cset"), None),
        P(("blk", "cset"), None),
        P("blk", "cset", None, None, None, None),
        P("blk", "cset", None, None),
        P("blk", "cset", None, None),
        P("blk", "cset", None),
        P(),
        P(),
    )
    out_specs = P("blk", "cset")
    return jax.shard_map(local, mesh=mesh, in_specs=in_specs, out_specs=out_specs, check_vma=False)
```

```python
import functools

import jax
import jax.numpy as jnp
from jax import lax
from jax.experimental import pallas as pl
from jax.experimental.pallas import tpu as pltpu
from jax.sharding import PartitionSpec as P

OUTPAD = 1024
TILE = 128
CHUNKS = 4
MESH = pl.DeviceIdType.MESH


def kernel(
    n_blk,
    n_cset,
    half,
    dst_s,
    src_s,
    count_s,
    active_h,
    passive_h,
    adjacency_h,
    left_h,
    right_h,
    out_ref,
    active_v,
    left_raw,
    right_raw,
    left_v,
    right_v,
    tiles_v,
    dense_v,
    picked_v,
    choose_v,
    neighbour_v,
    result_v,
    *rest,
):
    home = rest[: half + 1]
    away = (None,) + rest[half + 1 : 2 * half + 1]
    (
        local_sem,
        own_send,
        side_send,
        sibling_send,
        home_recv,
        away_recv,
        out_send,
        out_recv,
    ) = rest[2 * half + 1 :]
    b = lax.axis_index("blk")
    c = lax.axis_index("cset")
    rows, channels = active_v.shape
    splits, sets = left_raw.shape
    width = out_ref.shape[1]
    piece = min(width, 256)
    sign = 2 * (b % 2) - 1
    sibling = (b - sign, c)
    others = [(c + i) % n_cset for i in range(1, n_cset)]
    targets = [None] + [
        ((b + k * (1 - 2 * ((b - k + n_blk) % 2)) + n_blk) % n_blk, c) for k in range(1, half + 1)
    ]
    sources = [None] + [((b + sign * k + n_blk) % n_blk, c) for k in range(1, half + 1)]

    barrier = pltpu.get_barrier_semaphore()
    senders = sources[1:] + [sibling] + [(b, o) for o in others]
    for device in senders:
        pl.semaphore_signal(barrier, inc=1, device_id=device, device_id_type=MESH)

    mine = pl.ds(pl.multiple_of(c * rows, rows), rows)
    copies = [
        pltpu.make_async_copy(left_h, left_raw, local_sem.at[0]),
        pltpu.make_async_copy(right_h, right_raw, local_sem.at[1]),
        pltpu.make_async_copy(active_h, active_v, local_sem.at[2]),
        pltpu.make_async_copy(adjacency_h, tiles_v, local_sem.at[3]),
        pltpu.make_async_copy(passive_h, home[0].at[mine, :], local_sem.at[4]),
    ]
    for copy in copies:
        copy.start()
    pl.semaphore_wait(barrier, len(senders))

    size = rows // CHUNKS

    def part(cset, q=0, length=size):
        return pl.ds(pl.multiple_of(cset * rows + q * size, size), length)

    def send(src, dst, send_sem, recv_sem, device):
        copy = pltpu.make_async_remote_copy(
            src_ref=src,
            dst_ref=dst,
            send_sem=send_sem,
            recv_sem=recv_sem,
            device_id=device,
            device_id_type=MESH,
        )
        copy.start()

    def to_others(k, q):
        block = home[k].at[part(c, q), :]
        for i, other in enumerate(others):
            send(block, block, side_send.at[k, i, q], home_recv.at[k, c, q], (b, other))

    def to_sibling(k, cset, q):
        send(
            home[k].at[part(cset, q), :],
            away[k + 1].at[part(cset, q), :],
            sibling_send.at[k, cset, q],
            away_recv.at[k, cset, q],
            sibling,
        )

    def arrived(ref, cset, q, sem):
        block = ref.at[part(cset, q), :]
        pltpu.make_async_copy(block, block, sem).wait()

    copies[4].wait()
    def begin(q, carry):
        block = home[0].at[part(c, q), :]
        for k in range(half, 0, -1):
            goal = home[k].at[part(c, q), :]
            send(block, goal, own_send.at[k - 1, q], home_recv.at[k, c, q], targets[k])
        to_others(0, q)
        to_sibling(0, c, q)
        return carry

    lax.fori_loop(0, CHUNKS, begin, 0)

    copies[0].wait()
    copies[1].wait()
    left_v[...] = jnp.full(left_v.shape, -1, jnp.float32)
    right_v[...] = jnp.full(right_v.shape, -1, jnp.float32)
    left_v[:splits, :sets] = left_raw[...].astype(jnp.float32)
    right_v[:splits, :sets] = right_raw[...].astype(jnp.float32)
    copies[2].wait()
    copies[3].wait()

    def assemble(r, carry):
        for d in range(rows // TILE):
            for e in range(n_cset * rows // TILE):
                total = jnp.zeros((TILE, TILE), jnp.bfloat16)
                for t in range(tiles_v.shape[1]):
                    here = (dst_s[0, r, 0, t] == d) & (src_s[0, r, 0, t] == e) & (count_s[0, 0, r] > t)
                    total = total + jnp.where(here, tiles_v[r, t], jnp.zeros_like(total))
                dense_v[r, d * TILE : (d + 1) * TILE, e * TILE : (e + 1) * TILE] = total
        return carry

    channel = lax.broadcasted_iota(jnp.int32, (channels, 256), 0).astype(jnp.bfloat16)
    one, zero = jnp.ones(channel.shape, jnp.bfloat16), jnp.zeros(channel.shape, jnp.bfloat16)

    def one_hot(table, j, columns):
        row = jnp.broadcast_to(table[pl.ds(j, 1), columns], (16, 256)).astype(jnp.bfloat16)
        return jnp.where(jnp.concatenate([row] * (channels // 16), axis=0) == channel, one, zero)

    def pick(j):
        for at in range(0, OUTPAD, 256):
            columns = slice(at, at + 256)
            choose_v[j, :, columns] = one_hot(right_v, j, columns)
            picked = jnp.dot(
                active_v[...], one_hot(left_v, j, columns), preferred_element_type=jnp.float32
            )
            picked_v[j, :, columns] = picked.astype(jnp.bfloat16)

    def side_arrived(k, q):
        for other in others:
            arrived(home[k], other, q, home_recv.at[k, other, q])
            if k < half:
                to_sibling(k, other, q)

    def own_arrived(k, q):
        arrived(home[k], c, q, home_recv.at[k, c, q])
        to_others(k, q)
        if k < half:
            to_sibling(k, c, q)

    lead = CHUNKS * (half + 1)
    stages = lead + CHUNKS * (half - 1)
    first = max(splits - stages, 0)

    def advance(j, carry):
        pl.when(j < splits)(lambda: pick(j))
        i = j - first
        for k in range(1, half + 1):
            now = (i >= 0) & (i < lead) & (i % (half + 1) == k - 1)
            pl.when(now)(functools.partial(own_arrived, k, i // (half + 1)))
        now = (i >= 0) & (i < lead) & (i % (half + 1) == half)
        pl.when(now)(functools.partial(side_arrived, 0, i // (half + 1)))
        for k in range(1, half):
            start = lead + CHUNKS * (k - 1)
            now = (i >= start) & (i < start + CHUNKS)
            pl.when(now)(functools.partial(side_arrived, k, i - start))
        return carry

    lax.fori_loop(0, 2 * half + 1, assemble, 0)
    lax.fori_loop(0, first + stages, advance, 0)

    def times(r, ref):
        return jnp.dot(dense_v[r], ref[...], preferred_element_type=jnp.float32)

    total = times(half, home[0])
    for k in range(1, half):
        total = total + times(half + sign * k, home[k])
    for k in range(1, half + 1):
        for cset in [c] + others:
            for q in range(CHUNKS):
                arrived(away[k], cset, q, away_recv.at[k - 1, cset, q])
        total = total + times(half - sign * k, away[k])
    for q in range(CHUNKS):
        side_arrived(half, q)
    total = total + times(half + sign * half, home[half])
    neighbour_v[...] = total.astype(jnp.bfloat16)

    pieces = width // piece
    for i, owner in enumerate(others + [c]):

        def join(p, carry):
            columns = pl.ds(pl.multiple_of(owner * width + p * piece, piece), piece)
            inside = pl.ds(pl.multiple_of(p * piece, piece), piece)

            def step(g, total):
                for u in range(4):
                    j = g * 4 + u
                    found = jnp.dot(
                        neighbour_v[...],
                        choose_v[j, :, columns],
                        preferred_element_type=jnp.float32,
                    )
                    total = total + picked_v[j, :, columns].astype(jnp.float32) * found
                return total

            total = lax.fori_loop(0, splits // 4, step, jnp.zeros((rows, piece), jnp.float32))
            if i < n_cset - 1:
                result_v[i, :, inside] = total.astype(jnp.bfloat16)
                send(
                    result_v.at[i, :, inside],
                    out_ref.at[part(c, 0, rows), inside],
                    out_send.at[i, p],
                    out_recv.at[c, p],
                    (b, owner),
                )
            else:
                out_ref[part(c, 0, rows), inside] = total.astype(jnp.bfloat16)
            return carry

        lax.fori_loop(0, pieces, join, 0)

    def finish(q, carry):
        block = home[0].at[part(c, q), :]
        sems = [own_send.at[k, q] for k in range(half)]
        sems += [side_send.at[k, i, q] for k in range(half + 1) for i in range(n_cset - 1)]
        sems += [sibling_send.at[k, i, q] for k in range(half) for i in range(n_cset)]
        for sem in sems:
            pltpu.make_async_copy(block, block, sem).wait()
        return carry

    def finish_out(p, carry):
        inside = pl.ds(pl.multiple_of(p * piece, piece), piece)
        for i, other in enumerate(others):
            block = result_v.at[i, :, inside]
            pltpu.make_async_copy(block, block, out_send.at[i, p]).wait()
            block = out_ref.at[part(other, 0, rows), inside]
            pltpu.make_async_copy(block, block, out_recv.at[other, p]).wait()
        return carry

    lax.fori_loop(0, CHUNKS, finish, 0)
    lax.fori_loop(0, pieces, finish_out, 0)


def local(
    active_table,
    passive_table,
    adjacency,
    tile_dst,
    tile_src,
    tile_count,
    split_active,
    split_passive,
):
    n_blk, n_cset = lax.axis_size("blk"), lax.axis_size("cset")
    rows, channels = passive_table.shape
    tiles = adjacency[0, 0]
    reach, slots = tiles.shape[:2]
    half = (reach - 1) // 2
    splits, sets = split_active.shape
    width = OUTPAD // n_cset
    pieces = width // min(width, 256)
    hbm = pl.BlockSpec(memory_space=pl.ANY)
    smem = pl.BlockSpec(memory_space=pltpu.SMEM)
    bf16 = jnp.bfloat16
    dma = pltpu.SemaphoreType.DMA
    table = (-(-splits // 8) * 8, OUTPAD)
    return pl.pallas_call(
        functools.partial(kernel, n_blk, n_cset, half),
        out_shape=pltpu.VMEM((n_cset * rows, width), bf16),
        in_specs=[smem] * 3 + [hbm] * 5,
        out_specs=pl.BlockSpec(memory_space=pltpu.VMEM),
        scratch_shapes=[
            pltpu.VMEM((rows, channels), bf16),
            pltpu.VMEM((splits, sets), jnp.int32),
            pltpu.VMEM((splits, sets), jnp.int32),
            pltpu.VMEM(table, jnp.float32),
            pltpu.VMEM(table, jnp.float32),
            pltpu.VMEM((reach, slots, TILE, TILE), bf16),
            pltpu.VMEM((reach, rows, n_cset * rows), bf16),
            pltpu.VMEM((splits, rows, OUTPAD), bf16),
            pltpu.VMEM((splits, channels, OUTPAD), bf16),
            pltpu.VMEM((rows, channels), bf16),
            pltpu.VMEM((max(n_cset - 1, 1), rows, width), bf16),
        ]
        + [pltpu.VMEM((n_cset * rows, channels), bf16)] * (2 * half + 1)
        + [
            dma((5,)),
            dma((half, CHUNKS)),
            dma((half + 1, n_cset, CHUNKS)),
            dma((half, n_cset, CHUNKS)),
            dma((half + 1, n_cset, CHUNKS)),
            dma((half, n_cset, CHUNKS)),
            dma((n_cset, pieces)),
            dma((n_cset, pieces)),
        ],
        compiler_params=pltpu.CompilerParams(
            collective_id=0, has_side_effects=True, vmem_limit_bytes=56 * 1024 * 1024
        ),
    )(
        jnp.transpose(tile_dst, (0, 2, 1, 3)),
        jnp.transpose(tile_src, (0, 2, 1, 3)),
        tile_count,
        active_table,
        passive_table,
        tiles,
        split_active,
        split_passive,
    )


def solution(mesh):
    in_specs = (
        P(("blk", "cset"), None),
        P(("blk", "cset"), None),
        P("blk", "cset", None, None, None, None),
        P("blk", "cset", None, None),
        P("blk", "cset", None, None),
        P("blk", "cset", None),
        P(),
        P(),
    )
    out_specs = P("blk", "cset")
    return jax.shard_map(local, mesh=mesh, in_specs=in_specs, out_specs=out_specs, check_vma=False)
```

```python
import functools

import jax
import jax.numpy as jnp
from jax import lax
from jax.experimental import pallas as pl
from jax.experimental.pallas import tpu as pltpu
from jax.sharding import PartitionSpec as P

OUTPAD = 1024
TILE = 128
CHUNKS = 4
GROUP = 4
MESH = pl.DeviceIdType.MESH


def kernel(
    n_blk,
    n_cset,
    half,
    dst_s,
    src_s,
    count_s,
    active_h,
    passive_h,
    adjacency_h,
    left_h,
    right_h,
    out_ref,
    active_v,
    left_raw,
    right_raw,
    left_v,
    right_v,
    tiles_v,
    dense_v,
    picked_v,
    choose_v,
    neighbour_v,
    result_v,
    *rest,
):
    home = rest[: half + 1]
    away = (None,) + rest[half + 1 : 2 * half + 1]
    (
        local_sem,
        own_send,
        side_send,
        sibling_send,
        home_recv,
        away_recv,
        out_send,
        out_recv,
    ) = rest[2 * half + 1 :]
    b = lax.axis_index("blk")
    c = lax.axis_index("cset")
    rows, channels = active_v.shape
    splits, sets = left_raw.shape
    width = out_ref.shape[1]
    piece = min(width, 256)
    sign = 2 * (b % 2) - 1
    sibling = (b - sign, c)
    others = [(c + i) % n_cset for i in range(1, n_cset)]
    targets = [None] + [
        ((b + k * (1 - 2 * ((b - k + n_blk) % 2)) + n_blk) % n_blk, c) for k in range(1, half + 1)
    ]
    sources = [None] + [((b + sign * k + n_blk) % n_blk, c) for k in range(1, half + 1)]

    barrier = pltpu.get_barrier_semaphore()
    senders = sources[1:] + [sibling] + [(b, o) for o in others]
    for device in senders:
        pl.semaphore_signal(barrier, inc=1, device_id=device, device_id_type=MESH)

    mine = pl.ds(pl.multiple_of(c * rows, rows), rows)
    copies = [
        pltpu.make_async_copy(left_h, left_raw, local_sem.at[0]),
        pltpu.make_async_copy(right_h, right_raw, local_sem.at[1]),
        pltpu.make_async_copy(active_h, active_v, local_sem.at[2]),
        pltpu.make_async_copy(adjacency_h, tiles_v, local_sem.at[3]),
        pltpu.make_async_copy(passive_h, home[0].at[mine, :], local_sem.at[4]),
    ]
    for copy in copies:
        copy.start()
    pl.semaphore_wait(barrier, len(senders))

    size = rows // CHUNKS

    def part(cset, q=0, length=size):
        return pl.ds(pl.multiple_of(cset * rows + q * size, size), length)

    def send(src, dst, send_sem, recv_sem, device):
        copy = pltpu.make_async_remote_copy(
            src_ref=src,
            dst_ref=dst,
            send_sem=send_sem,
            recv_sem=recv_sem,
            device_id=device,
            device_id_type=MESH,
        )
        copy.start()

    def to_others(k, q):
        block = home[k].at[part(c, q), :]
        for i, other in enumerate(others):
            send(block, block, side_send.at[k, i, q], home_recv.at[k, c, q], (b, other))

    def to_sibling(k, cset, q):
        send(
            home[k].at[part(cset, q), :],
            away[k + 1].at[part(cset, q), :],
            sibling_send.at[k, cset, q],
            away_recv.at[k, cset, q],
            sibling,
        )

    def arrived(ref, cset, q, sem):
        block = ref.at[part(cset, q), :]
        pltpu.make_async_copy(block, block, sem).wait()

    copies[4].wait()
    def begin(q, carry):
        block = home[0].at[part(c, q), :]
        for k in range(half, 0, -1):
            goal = home[k].at[part(c, q), :]
            send(block, goal, own_send.at[k - 1, q], home_recv.at[k, c, q], targets[k])
        to_others(0, q)
        to_sibling(0, c, q)
        return carry

    lax.fori_loop(0, CHUNKS, begin, 0)

    copies[0].wait()
    copies[1].wait()
    left_v[...] = jnp.full(left_v.shape, -1, jnp.float32)
    right_v[...] = jnp.full(right_v.shape, -1, jnp.float32)
    left_v[:splits, :sets] = left_raw[...].astype(jnp.float32)
    right_v[:splits, :sets] = right_raw[...].astype(jnp.float32)
    copies[2].wait()
    copies[3].wait()

    def assemble(r):
        for d in range(rows // TILE):
            for e in range(n_cset * rows // TILE):
                total = jnp.zeros((TILE, TILE), jnp.bfloat16)
                for t in range(tiles_v.shape[1]):
                    here = (dst_s[0, r, 0, t] == d) & (src_s[0, r, 0, t] == e) & (count_s[0, 0, r] > t)
                    total = total + jnp.where(here, tiles_v[r, t], jnp.zeros_like(total))
                dense_v[r, d * TILE : (d + 1) * TILE, e * TILE : (e + 1) * TILE] = total

    channel = lax.broadcasted_iota(jnp.int32, (channels, 256), 0).astype(jnp.bfloat16)
    one, zero = jnp.ones(channel.shape, jnp.bfloat16), jnp.zeros(channel.shape, jnp.bfloat16)

    def one_hot(table, j, columns):
        row = jnp.broadcast_to(table[pl.ds(j, 1), columns], (16, 256)).astype(jnp.bfloat16)
        return jnp.where(jnp.concatenate([row] * (channels // 16), axis=0) == channel, one, zero)

    def pick(start):
        for j in range(GROUP):
            for at in range(0, OUTPAD, 256):
                columns = slice(at, at + 256)
                choose_v[start + j, :, columns] = one_hot(right_v, start + j, columns)
                picked = jnp.dot(
                    active_v[...],
                    one_hot(left_v, start + j, columns),
                    preferred_element_type=jnp.float32,
                )
                picked_v[start + j, :, columns] = picked.astype(jnp.bfloat16)

    def side_arrived(k, q):
        for other in others:
            arrived(home[k], other, q, home_recv.at[k, other, q])
            if k < half:
                to_sibling(k, other, q)

    def own_arrived(k, q):
        arrived(home[k], c, q, home_recv.at[k, c, q])
        to_others(k, q)
        if k < half:
            to_sibling(k, c, q)

    groups = splits // GROUP
    reach = 2 * half + 1

    def advance(g, carry):
        pl.when(g < groups)(functools.partial(pick, g * GROUP))
        pl.when(g < reach)(functools.partial(assemble, g))

        @pl.when((g >= 1) & (g <= CHUNKS))
        def _():
            for k in range(1, half + 1):
                own_arrived(k, g - 1)
            side_arrived(0, g - 1)

        return carry

    lax.fori_loop(0, max(groups, reach, CHUNKS + 1), advance, 0)

    def forward(q, carry):
        for k in range(1, half):
            side_arrived(k, q)
        return carry

    lax.fori_loop(0, CHUNKS, forward, 0)

    def times(r, ref):
        return jnp.dot(dense_v[r], ref[...], preferred_element_type=jnp.float32)

    total = times(half, home[0])
    for k in range(1, half):
        total = total + times(half + sign * k, home[k])
    for k in range(1, half + 1):
        for cset in [c] + others:
            for q in range(CHUNKS):
                arrived(away[k], cset, q, away_recv.at[k - 1, cset, q])
        total = total + times(half - sign * k, away[k])
    for q in range(CHUNKS):
        side_arrived(half, q)
    total = total + times(half + sign * half, home[half])
    neighbour_v[...] = total.astype(jnp.bfloat16)

    pieces = width // piece

    def join(n, carry):
        i, p = n // pieces, n % pieces
        owner = (c + 1 + i) % n_cset
        columns = pl.ds(pl.multiple_of(owner * width + p * piece, piece), piece)
        inside = pl.ds(pl.multiple_of(p * piece, piece), piece)
        total = jnp.zeros((rows, piece), jnp.float32)
        for j in range(splits):
            found = jnp.dot(
                neighbour_v[...], choose_v[j, :, columns], preferred_element_type=jnp.float32
            )
            total = total + picked_v[j, :, columns].astype(jnp.float32) * found
        result_v[i, :, inside] = total.astype(jnp.bfloat16)

        @pl.when(i < n_cset - 1)
        def _():
            send(
                result_v.at[i, :, inside],
                out_ref.at[part(c, 0, rows), inside],
                out_send.at[i, p],
                out_recv.at[c, p],
                (b, owner),
            )

        @pl.when(i == n_cset - 1)
        def _():
            out_ref[part(c, 0, rows), inside] = result_v[i, :, inside]

        return carry

    lax.fori_loop(0, n_cset * pieces, join, 0)

    def finish(q, carry):
        block = home[0].at[part(c, q), :]
        sems = [own_send.at[k, q] for k in range(half)]
        sems += [side_send.at[k, i, q] for k in range(half + 1) for i in range(n_cset - 1)]
        sems += [sibling_send.at[k, i, q] for k in range(half) for i in range(n_cset)]
        for sem in sems:
            pltpu.make_async_copy(block, block, sem).wait()
        return carry

    def finish_out(p, carry):
        inside = pl.ds(pl.multiple_of(p * piece, piece), piece)
        for i, other in enumerate(others):
            block = result_v.at[i, :, inside]
            pltpu.make_async_copy(block, block, out_send.at[i, p]).wait()
            block = out_ref.at[part(other, 0, rows), inside]
            pltpu.make_async_copy(block, block, out_recv.at[other, p]).wait()
        return carry

    lax.fori_loop(0, CHUNKS, finish, 0)
    lax.fori_loop(0, pieces, finish_out, 0)


def local(
    active_table,
    passive_table,
    adjacency,
    tile_dst,
    tile_src,
    tile_count,
    split_active,
    split_passive,
):
    n_blk, n_cset = lax.axis_size("blk"), lax.axis_size("cset")
    rows, channels = passive_table.shape
    tiles = adjacency[0, 0]
    reach, slots = tiles.shape[:2]
    half = (reach - 1) // 2
    splits, sets = split_active.shape
    width = OUTPAD // n_cset
    pieces = width // min(width, 256)
    hbm = pl.BlockSpec(memory_space=pl.ANY)
    smem = pl.BlockSpec(memory_space=pltpu.SMEM)
    bf16 = jnp.bfloat16
    dma = pltpu.SemaphoreType.DMA
    table = (-(-splits // 8) * 8, OUTPAD)
    return pl.pallas_call(
        functools.partial(kernel, n_blk, n_cset, half),
        out_shape=pltpu.VMEM((n_cset * rows, width), bf16),
        in_specs=[smem] * 3 + [hbm] * 5,
        out_specs=pl.BlockSpec(memory_space=pltpu.VMEM),
        scratch_shapes=[
            pltpu.VMEM((rows, channels), bf16),
            pltpu.VMEM((splits, sets), jnp.int32),
            pltpu.VMEM((splits, sets), jnp.int32),
            pltpu.VMEM(table, jnp.float32),
            pltpu.VMEM(table, jnp.float32),
            pltpu.VMEM((reach, slots, TILE, TILE), bf16),
            pltpu.VMEM((reach, rows, n_cset * rows), bf16),
            pltpu.VMEM((splits, rows, OUTPAD), bf16),
            pltpu.VMEM((splits, channels, OUTPAD), bf16),
            pltpu.VMEM((rows, channels), bf16),
            pltpu.VMEM((n_cset, rows, width), bf16),
        ]
        + [pltpu.VMEM((n_cset * rows, channels), bf16)] * (2 * half + 1)
        + [
            dma((5,)),
            dma((half, CHUNKS)),
            dma((half + 1, n_cset, CHUNKS)),
            dma((half, n_cset, CHUNKS)),
            dma((half + 1, n_cset, CHUNKS)),
            dma((half, n_cset, CHUNKS)),
            dma((n_cset, pieces)),
            dma((n_cset, pieces)),
        ],
        compiler_params=pltpu.CompilerParams(
            collective_id=0, has_side_effects=True, vmem_limit_bytes=56 * 1024 * 1024
        ),
    )(
        jnp.transpose(tile_dst, (0, 2, 1, 3)),
        jnp.transpose(tile_src, (0, 2, 1, 3)),
        tile_count,
        active_table,
        passive_table,
        tiles,
        split_active,
        split_passive,
    )


def solution(mesh):
    in_specs = (
        P(("blk", "cset"), None),
        P(("blk", "cset"), None),
        P("blk", "cset", None, None, None, None),
        P("blk", "cset", None, None),
        P("blk", "cset", None, None),
        P("blk", "cset", None),
        P(),
        P(),
    )
    out_specs = P("blk", "cset")
    return jax.shard_map(local, mesh=mesh, in_specs=in_specs, out_specs=out_specs, check_vma=False)
```

```python
import functools

import jax
import jax.numpy as jnp
from jax import lax
from jax.experimental import pallas as pl
from jax.experimental.pallas import tpu as pltpu
from jax.sharding import PartitionSpec as P

OUTPAD = 1024
TILE = 128
CHUNKS = 4
GROUP = 4
MESH = pl.DeviceIdType.MESH


def kernel(
    n_blk,
    n_cset,
    half,
    dst_s,
    src_s,
    count_s,
    active_h,
    passive_h,
    adjacency_h,
    left_h,
    right_h,
    out_ref,
    active_v,
    left_raw,
    right_raw,
    left_v,
    right_v,
    left_own,
    right_own,
    tiles_v,
    dense_v,
    picked_v,
    choose_left_v,
    choose_right_v,
    neighbour_v,
    *rest,
):
    home = rest[: half + 1]
    away = (None,) + rest[half + 1 : 2 * half + 1]
    (
        local_sem,
        own_send,
        side_send,
        sibling_send,
        home_recv,
        away_recv,
        far_send,
        active_send,
        active_recv,
        sum_send,
        sum_recv,
    ) = rest[2 * half + 1 :]
    b = lax.axis_index("blk")
    c = lax.axis_index("cset")
    channels = active_v.shape[1]
    rows = active_v.shape[0] // n_cset
    splits, sets = left_raw.shape
    width = out_ref.shape[1]
    piece = min(width, 256)
    sign = 2 * (b % 2) - 1
    sibling = (b - sign, c)
    others = [(c + i) % n_cset for i in range(1, n_cset)]
    targets = [None] + [
        ((b + k * (1 - 2 * ((b - k + n_blk) % 2)) + n_blk) % n_blk, c) for k in range(1, half + 1)
    ]
    sources = [None] + [((b + sign * k + n_blk) % n_blk, c) for k in range(1, half + 1)]

    barrier = pltpu.get_barrier_semaphore()
    senders = sources[1:] + [sibling] + [(b, o) for o in others]
    for device in senders:
        pl.semaphore_signal(barrier, inc=1, device_id=device, device_id_type=MESH)

    mine = pl.ds(pl.multiple_of(c * rows, rows), rows)
    copies = [
        pltpu.make_async_copy(left_h, left_raw, local_sem.at[0]),
        pltpu.make_async_copy(right_h, right_raw, local_sem.at[1]),
        pltpu.make_async_copy(active_h, active_v.at[mine, :], local_sem.at[2]),
        pltpu.make_async_copy(adjacency_h, tiles_v, local_sem.at[3]),
        pltpu.make_async_copy(passive_h, home[0].at[mine, :], local_sem.at[4]),
    ]
    for copy in copies:
        copy.start()
    pl.semaphore_wait(barrier, len(senders))

    size = rows // CHUNKS

    def part(cset, q=0, length=size):
        return pl.ds(pl.multiple_of(cset * rows + q * size, size), length)

    def send(src, dst, send_sem, recv_sem, device):
        copy = pltpu.make_async_remote_copy(
            src_ref=src,
            dst_ref=dst,
            send_sem=send_sem,
            recv_sem=recv_sem,
            device_id=device,
            device_id_type=MESH,
        )
        copy.start()

    def to_others(k, q):
        block = home[k].at[part(c, q), :]
        for i, other in enumerate(others):
            send(block, block, side_send.at[k, i, q], home_recv.at[k, c, q], (b, other))

    def to_sibling(k, cset, q):
        send(
            home[k].at[part(cset, q), :],
            away[k + 1].at[part(cset, q), :],
            sibling_send.at[k, cset, q],
            away_recv.at[k, cset, q],
            sibling,
        )

    def arrived(ref, cset, q, sem):
        block = ref.at[part(cset, q), :]
        pltpu.make_async_copy(block, block, sem).wait()

    copies[4].wait()
    def begin(q, carry):
        block = home[0].at[part(c, q), :]
        for k in range(half, 0, -1):
            goal = home[k].at[part(c, q), :]
            send(block, goal, own_send.at[k - 1, q], home_recv.at[k, c, q], targets[k])
        to_others(0, q)
        to_sibling(0, c, q)
        return carry

    lax.fori_loop(0, CHUNKS, begin, 0)

    copies[0].wait()
    copies[1].wait()
    left_v[...] = jnp.full(left_v.shape, -1, jnp.float32)
    right_v[...] = jnp.full(right_v.shape, -1, jnp.float32)
    left_v[:splits, :sets] = left_raw[...].astype(jnp.float32)
    right_v[:splits, :sets] = right_raw[...].astype(jnp.float32)
    own_columns = pl.ds(pl.multiple_of(c * width, width), width)
    left_own[...] = left_v[:, own_columns]
    right_own[...] = right_v[:, own_columns]
    copies[2].wait()
    copies[3].wait()

    def assemble(r):
        for d in range(rows // TILE):
            for e in range(n_cset * rows // TILE):
                total = jnp.zeros((TILE, TILE), jnp.bfloat16)
                for t in range(tiles_v.shape[1]):
                    here = (dst_s[0, r, 0, t] == d) & (src_s[0, r, 0, t] == e) & (count_s[0, 0, r] > t)
                    total = total + jnp.where(here, tiles_v[r, t], jnp.zeros_like(total))
                dense_v[r, d * TILE : (d + 1) * TILE, e * TILE : (e + 1) * TILE] = total

    channel = lax.broadcasted_iota(jnp.int32, (channels, piece), 0).astype(jnp.bfloat16)
    one, zero = jnp.ones(channel.shape, jnp.bfloat16), jnp.zeros(channel.shape, jnp.bfloat16)

    def one_hot(table, j, columns):
        row = jnp.broadcast_to(table[pl.ds(j, 1), columns], (16, piece)).astype(jnp.bfloat16)
        return jnp.where(jnp.concatenate([row] * (channels // 16), axis=0) == channel, one, zero)

    def pick(start):
        for j in range(GROUP):
            for at in range(0, width, piece):
                inside = slice(at, at + piece)
                left = one_hot(left_own, start + j, inside)
                choose_left_v[start + j, :, inside] = left
                choose_right_v[start + j, :, inside] = one_hot(right_own, start + j, inside)
                picked = jnp.dot(active_v[mine, :], left, preferred_element_type=jnp.float32)
                picked_v[start + j, mine, inside] = picked.astype(jnp.bfloat16)

    def pick_others(start):
        for other in others:
            there = part(other, 0, rows)
            for j in range(GROUP):
                for at in range(0, width, piece):
                    inside = slice(at, at + piece)
                    picked = jnp.dot(
                        active_v[there, :],
                        choose_left_v[start + j, :, inside],
                        preferred_element_type=jnp.float32,
                    )
                    picked_v[start + j, there, inside] = picked.astype(jnp.bfloat16)

    def side_arrived(k, q):
        for other in others:
            arrived(home[k], other, q, home_recv.at[k, other, q])
            if k == 0:
                send(
                    home[0].at[part(other, q), :],
                    home[half].at[part(other, q), :],
                    far_send.at[other, q],
                    home_recv.at[half, other, q],
                    targets[half],
                )
            if k < half:
                to_sibling(k, other, q)

    def own_arrived(k, q):
        arrived(home[k], c, q, home_recv.at[k, c, q])
        if k < half:
            to_others(k, q)
            to_sibling(k, c, q)

    groups = splits // GROUP
    reach = 2 * half + 1

    def advance(g, carry):
        pl.when(g < groups)(functools.partial(pick, g * GROUP))

        @pl.when((g >= 1) & (g <= CHUNKS))
        def _():
            side_arrived(0, g - 1)
            for k in range(1, half + 1):
                own_arrived(k, g - 1)

        @pl.when(g == 1)
        def _():
            for i, other in enumerate(others):
                block = active_v.at[mine, :]
                send(block, block, active_send.at[i], active_recv.at[c], (b, other))

        pl.when(g < reach)(functools.partial(assemble, g))
        return carry

    lax.fori_loop(0, max(groups, reach, CHUNKS + 1), advance, 0)
    for other in others:
        block = active_v.at[part(other, 0, rows), :]
        pltpu.make_async_copy(block, block, active_recv.at[other]).wait()

    def forward(g, carry):
        pl.when(g < groups)(functools.partial(pick_others, g * GROUP))

        @pl.when(g < CHUNKS)
        def _():
            for k in range(1, half):
                side_arrived(k, g)

        return carry

    lax.fori_loop(0, max(groups, CHUNKS), forward, 0)

    def times(r, ref):
        return jnp.dot(dense_v[r], ref[...], preferred_element_type=jnp.float32)

    total = times(half, home[0])
    for k in range(1, half):
        total = total + times(half + sign * k, home[k])
    for k in range(1, half + 1):
        for cset in [c] + others:
            for q in range(CHUNKS):
                arrived(away[k], cset, q, away_recv.at[k - 1, cset, q])
        total = total + times(half - sign * k, away[k])
    for q in range(CHUNKS):
        side_arrived(half, q)
    total = total + times(half + sign * half, home[half])
    neighbour_v[mine, :] = total.astype(jnp.bfloat16)
    for i, other in enumerate(others):
        block = neighbour_v.at[mine, :]
        send(block, block, sum_send.at[i], sum_recv.at[c], (b, other))
    pieces = width // piece

    def join(n, carry):
        i, p = n // pieces, n % pieces
        owner = (c + i) % n_cset
        there = part(owner, 0, rows)
        inside = pl.ds(pl.multiple_of(p * piece, piece), piece)

        @pl.when((i > 0) & (p == 0))
        def _():
            block = neighbour_v.at[there, :]
            pltpu.make_async_copy(block, block, sum_recv.at[owner]).wait()

        total = jnp.zeros((rows, piece), jnp.float32)
        for j in range(splits):
            found = jnp.dot(
                neighbour_v[there, :],
                choose_right_v[j, :, inside],
                preferred_element_type=jnp.float32,
            )
            total = total + picked_v[j, there, inside].astype(jnp.float32) * found
        out_ref[there, inside] = total.astype(jnp.bfloat16)
        return carry

    lax.fori_loop(0, n_cset * pieces, join, 0)

    def finish(q, carry):
        block = home[0].at[part(c, q), :]
        sems = [own_send.at[k, q] for k in range(half)]
        sems += [side_send.at[k, i, q] for k in range(half) for i in range(n_cset - 1)]
        sems += [sibling_send.at[k, i, q] for k in range(half) for i in range(n_cset)]
        sems += [far_send.at[other, q] for other in others]
        for sem in sems:
            pltpu.make_async_copy(block, block, sem).wait()
        return carry

    lax.fori_loop(0, CHUNKS, finish, 0)
    for i in range(n_cset - 1):
        block = active_v.at[mine, :]
        pltpu.make_async_copy(block, block, active_send.at[i]).wait()
        block = neighbour_v.at[mine, :]
        pltpu.make_async_copy(block, block, sum_send.at[i]).wait()


def local(
    active_table,
    passive_table,
    adjacency,
    tile_dst,
    tile_src,
    tile_count,
    split_active,
    split_passive,
):
    n_blk, n_cset = lax.axis_size("blk"), lax.axis_size("cset")
    rows, channels = passive_table.shape
    tiles = adjacency[0, 0]
    reach, slots = tiles.shape[:2]
    half = (reach - 1) // 2
    splits, sets = split_active.shape
    width = OUTPAD // n_cset
    hbm = pl.BlockSpec(memory_space=pl.ANY)
    smem = pl.BlockSpec(memory_space=pltpu.SMEM)
    bf16 = jnp.bfloat16
    dma = pltpu.SemaphoreType.DMA
    table = (-(-splits // 8) * 8, OUTPAD)
    return pl.pallas_call(
        functools.partial(kernel, n_blk, n_cset, half),
        out_shape=pltpu.VMEM((n_cset * rows, width), bf16),
        in_specs=[smem] * 3 + [hbm] * 5,
        out_specs=pl.BlockSpec(memory_space=pltpu.VMEM),
        scratch_shapes=[
            pltpu.VMEM((n_cset * rows, channels), bf16),
            pltpu.VMEM((splits, sets), jnp.int32),
            pltpu.VMEM((splits, sets), jnp.int32),
            pltpu.VMEM(table, jnp.float32),
            pltpu.VMEM(table, jnp.float32),
            pltpu.VMEM((table[0], width), jnp.float32),
            pltpu.VMEM((table[0], width), jnp.float32),
            pltpu.VMEM((reach, slots, TILE, TILE), bf16),
            pltpu.VMEM((reach, rows, n_cset * rows), bf16),
            pltpu.VMEM((splits, n_cset * rows, width), bf16),
            pltpu.VMEM((splits, channels, width), bf16),
            pltpu.VMEM((splits, channels, width), bf16),
            pltpu.VMEM((n_cset * rows, channels), bf16),
        ]
        + [pltpu.VMEM((n_cset * rows, channels), bf16)] * (2 * half + 1)
        + [
            dma((5,)),
            dma((half, CHUNKS)),
            dma((half + 1, n_cset, CHUNKS)),
            dma((half, n_cset, CHUNKS)),
            dma((half + 1, n_cset, CHUNKS)),
            dma((half, n_cset, CHUNKS)),
            dma((n_cset, CHUNKS)),
            dma((n_cset,)),
            dma((n_cset,)),
            dma((n_cset,)),
            dma((n_cset,)),
        ],
        compiler_params=pltpu.CompilerParams(
            collective_id=0, has_side_effects=True, vmem_limit_bytes=56 * 1024 * 1024
        ),
    )(
        jnp.transpose(tile_dst, (0, 2, 1, 3)),
        jnp.transpose(tile_src, (0, 2, 1, 3)),
        tile_count,
        active_table,
        passive_table,
        tiles,
        split_active,
        split_passive,
    )


def solution(mesh):
    in_specs = (
        P(("blk", "cset"), None),
        P(("blk", "cset"), None),
        P("blk", "cset", None, None, None, None),
        P("blk", "cset", None, None),
        P("blk", "cset", None, None),
        P("blk", "cset", None),
        P(),
        P(),
    )
    out_specs = P("blk", "cset")
    return jax.shard_map(local, mesh=mesh, in_specs=in_specs, out_specs=out_specs, check_vma=False)
```

```python
import functools

import jax
import jax.numpy as jnp
from jax import lax
from jax.experimental import pallas as pl
from jax.experimental.pallas import tpu as pltpu
from jax.sharding import PartitionSpec as P

OUTPAD = 1024
TILE = 128
CHUNKS = 4
GROUP = 4
MESH = pl.DeviceIdType.MESH


def kernel(
    n_blk,
    n_cset,
    half,
    dst_s,
    src_s,
    count_s,
    active_h,
    passive_h,
    adjacency_h,
    left_h,
    right_h,
    out_ref,
    active_v,
    left_raw,
    right_raw,
    left_v,
    right_v,
    left_own,
    right_own,
    tiles_v,
    dense_v,
    picked_v,
    choose_left_v,
    choose_right_v,
    neighbour_v,
    *rest,
):
    home = rest[: half + 1]
    away = (None,) + rest[half + 1 : 2 * half + 1]
    (
        local_sem,
        tile_sem,
        own_send,
        side_send,
        sibling_send,
        home_recv,
        away_recv,
        far_send,
        active_send,
        active_recv,
        sum_send,
        sum_recv,
    ) = rest[2 * half + 1 :]
    b = lax.axis_index("blk")
    c = lax.axis_index("cset")
    channels = active_v.shape[1]
    rows = active_v.shape[0] // n_cset
    splits, sets = left_raw.shape
    width = out_ref.shape[1]
    piece = min(width, 256)
    sign = 2 * (b % 2) - 1
    sibling = (b - sign, c)
    others = [(c + i) % n_cset for i in range(1, n_cset)]
    targets = [None] + [
        ((b + k * (1 - 2 * ((b - k + n_blk) % 2)) + n_blk) % n_blk, c) for k in range(1, half + 1)
    ]
    sources = [None] + [((b + sign * k + n_blk) % n_blk, c) for k in range(1, half + 1)]

    barrier = pltpu.get_barrier_semaphore()
    senders = sources[1:] + [sibling] + [(b, o) for o in others]
    for device in senders:
        pl.semaphore_signal(barrier, inc=1, device_id=device, device_id_type=MESH)

    mine = pl.ds(pl.multiple_of(c * rows, rows), rows)
    copies = [
        pltpu.make_async_copy(left_h, left_raw, local_sem.at[0]),
        pltpu.make_async_copy(right_h, right_raw, local_sem.at[1]),
        pltpu.make_async_copy(active_h, active_v.at[mine, :], local_sem.at[2]),
        pltpu.make_async_copy(passive_h, home[0].at[mine, :], local_sem.at[3]),
    ]
    for copy in copies[::-1]:
        copy.start()

    def fetch(r):
        return pltpu.make_async_copy(adjacency_h.at[r], tiles_v.at[r], tile_sem.at[r])

    for r in range(2 * half + 1):
        fetch(r).start()
    pl.semaphore_wait(barrier, len(senders))

    size = rows // CHUNKS

    def part(cset, q=0, length=size):
        return pl.ds(pl.multiple_of(cset * rows + q * size, size), length)

    def send(src, dst, send_sem, recv_sem, device):
        copy = pltpu.make_async_remote_copy(
            src_ref=src,
            dst_ref=dst,
            send_sem=send_sem,
            recv_sem=recv_sem,
            device_id=device,
            device_id_type=MESH,
        )
        copy.start()

    def to_others(k, q):
        block = home[k].at[part(c, q), :]
        for i, other in enumerate(others):
            send(block, block, side_send.at[k, i, q], home_recv.at[k, c, q], (b, other))

    def to_sibling(k, cset, q):
        send(
            home[k].at[part(cset, q), :],
            away[k + 1].at[part(cset, q), :],
            sibling_send.at[k, cset, q],
            away_recv.at[k, cset, q],
            sibling,
        )

    def arrived(ref, cset, q, sem):
        block = ref.at[part(cset, q), :]
        pltpu.make_async_copy(block, block, sem).wait()

    copies[3].wait()
    def begin(q, carry):
        block = home[0].at[part(c, q), :]
        for k in range(half, 0, -1):
            goal = home[k].at[part(c, q), :]
            send(block, goal, own_send.at[k - 1, q], home_recv.at[k, c, q], targets[k])
        to_others(0, q)
        to_sibling(0, c, q)
        return carry

    lax.fori_loop(0, CHUNKS, begin, 0)

    copies[0].wait()
    copies[1].wait()
    left_v[...] = jnp.full(left_v.shape, -1, jnp.float32)
    right_v[...] = jnp.full(right_v.shape, -1, jnp.float32)
    left_v[:splits, :sets] = left_raw[...].astype(jnp.float32)
    right_v[:splits, :sets] = right_raw[...].astype(jnp.float32)
    own_columns = pl.ds(pl.multiple_of(c * width, width), width)
    left_own[...] = left_v[:, own_columns]
    right_own[...] = right_v[:, own_columns]
    copies[2].wait()

    def assemble(r):
        fetch(r).wait()
        for d in range(rows // TILE):
            for e in range(n_cset * rows // TILE):
                total = jnp.zeros((TILE, TILE), jnp.bfloat16)
                for t in range(tiles_v.shape[1]):
                    here = (dst_s[0, r, 0, t] == d) & (src_s[0, r, 0, t] == e) & (count_s[0, 0, r] > t)
                    total = total + jnp.where(here, tiles_v[r, t], jnp.zeros_like(total))
                dense_v[r, d * TILE : (d + 1) * TILE, e * TILE : (e + 1) * TILE] = total

    channel = lax.broadcasted_iota(jnp.int32, (channels, piece), 0).astype(jnp.bfloat16)
    one, zero = jnp.ones(channel.shape, jnp.bfloat16), jnp.zeros(channel.shape, jnp.bfloat16)

    def one_hot(table, j, columns):
        row = jnp.broadcast_to(table[pl.ds(j, 1), columns], (16, piece)).astype(jnp.bfloat16)
        return jnp.where(jnp.concatenate([row] * (channels // 16), axis=0) == channel, one, zero)

    def pick(start):
        for j in range(GROUP):
            for at in range(0, width, piece):
                inside = slice(at, at + piece)
                left = one_hot(left_own, start + j, inside)
                choose_left_v[start + j, :, inside] = left
                choose_right_v[start + j, :, inside] = one_hot(right_own, start + j, inside)
                picked = jnp.dot(active_v[mine, :], left, preferred_element_type=jnp.float32)
                picked_v[start + j, mine, inside] = picked.astype(jnp.bfloat16)

    def pick_others(start):
        for other in others:
            there = part(other, 0, rows)
            for j in range(GROUP):
                for at in range(0, width, piece):
                    inside = slice(at, at + piece)
                    picked = jnp.dot(
                        active_v[there, :],
                        choose_left_v[start + j, :, inside],
                        preferred_element_type=jnp.float32,
                    )
                    picked_v[start + j, there, inside] = picked.astype(jnp.bfloat16)

    def side_arrived(k, q):
        for other in others:
            arrived(home[k], other, q, home_recv.at[k, other, q])
            if k == 0:
                send(
                    home[0].at[part(other, q), :],
                    home[half].at[part(other, q), :],
                    far_send.at[other, q],
                    home_recv.at[half, other, q],
                    targets[half],
                )
            if k < half:
                to_sibling(k, other, q)

    def own_arrived(k, q):
        arrived(home[k], c, q, home_recv.at[k, c, q])
        if k < half:
            to_others(k, q)
            to_sibling(k, c, q)

    groups = splits // GROUP
    reach = 2 * half + 1

    def advance(g, carry):
        pl.when(g < groups)(functools.partial(pick, g * GROUP))

        @pl.when((g >= 1) & (g <= CHUNKS))
        def _():
            side_arrived(0, g - 1)
            for k in range(1, half + 1):
                own_arrived(k, g - 1)

        @pl.when(g == 1)
        def _():
            for i, other in enumerate(others):
                block = active_v.at[mine, :]
                send(block, block, active_send.at[i], active_recv.at[c], (b, other))

        pl.when(g < reach)(functools.partial(assemble, g))
        return carry

    lax.fori_loop(0, max(groups, reach, CHUNKS + 1), advance, 0)
    for other in others:
        block = active_v.at[part(other, 0, rows), :]
        pltpu.make_async_copy(block, block, active_recv.at[other]).wait()

    def forward(g, carry):
        pl.when(g < groups)(functools.partial(pick_others, g * GROUP))

        @pl.when(g < CHUNKS)
        def _():
            for k in range(1, half):
                side_arrived(k, g)

        return carry

    lax.fori_loop(0, max(groups, CHUNKS), forward, 0)

    def times(r, ref):
        return jnp.dot(dense_v[r], ref[...], preferred_element_type=jnp.float32)

    total = times(half, home[0])
    for k in range(1, half):
        total = total + times(half + sign * k, home[k])
    for k in range(1, half + 1):
        for cset in [c] + others:
            for q in range(CHUNKS):
                arrived(away[k], cset, q, away_recv.at[k - 1, cset, q])
        total = total + times(half - sign * k, away[k])
    for q in range(CHUNKS):
        side_arrived(half, q)
    total = total + times(half + sign * half, home[half])
    neighbour_v[mine, :] = total.astype(jnp.bfloat16)
    for i, other in enumerate(others):
        block = neighbour_v.at[mine, :]
        send(block, block, sum_send.at[i], sum_recv.at[c], (b, other))
    pieces = width // piece

    def join(n, carry):
        i, p = n // pieces, n % pieces
        owner = (c + i) % n_cset
        there = part(owner, 0, rows)
        inside = pl.ds(pl.multiple_of(p * piece, piece), piece)

        @pl.when((i > 0) & (p == 0))
        def _():
            block = neighbour_v.at[there, :]
            pltpu.make_async_copy(block, block, sum_recv.at[owner]).wait()

        total = jnp.zeros((rows, piece), jnp.float32)
        for j in range(splits):
            found = jnp.dot(
                neighbour_v[there, :],
                choose_right_v[j, :, inside],
                preferred_element_type=jnp.float32,
            )
            total = total + picked_v[j, there, inside].astype(jnp.float32) * found
        out_ref[there, inside] = total.astype(jnp.bfloat16)
        return carry

    lax.fori_loop(0, n_cset * pieces, join, 0)

    def finish(q, carry):
        block = home[0].at[part(c, q), :]
        sems = [own_send.at[k, q] for k in range(half)]
        sems += [side_send.at[k, i, q] for k in range(half) for i in range(n_cset - 1)]
        sems += [sibling_send.at[k, i, q] for k in range(half) for i in range(n_cset)]
        sems += [far_send.at[other, q] for other in others]
        for sem in sems:
            pltpu.make_async_copy(block, block, sem).wait()
        return carry

    lax.fori_loop(0, CHUNKS, finish, 0)
    for i in range(n_cset - 1):
        block = active_v.at[mine, :]
        pltpu.make_async_copy(block, block, active_send.at[i]).wait()
        block = neighbour_v.at[mine, :]
        pltpu.make_async_copy(block, block, sum_send.at[i]).wait()


def local(
    active_table,
    passive_table,
    adjacency,
    tile_dst,
    tile_src,
    tile_count,
    split_active,
    split_passive,
):
    n_blk, n_cset = lax.axis_size("blk"), lax.axis_size("cset")
    rows, channels = passive_table.shape
    tiles = adjacency[0, 0]
    reach, slots = tiles.shape[:2]
    half = (reach - 1) // 2
    splits, sets = split_active.shape
    width = OUTPAD // n_cset
    hbm = pl.BlockSpec(memory_space=pl.ANY)
    smem = pl.BlockSpec(memory_space=pltpu.SMEM)
    bf16 = jnp.bfloat16
    dma = pltpu.SemaphoreType.DMA
    table = (-(-splits // 8) * 8, OUTPAD)
    return pl.pallas_call(
        functools.partial(kernel, n_blk, n_cset, half),
        out_shape=pltpu.VMEM((n_cset * rows, width), bf16),
        in_specs=[smem] * 3 + [hbm] * 5,
        out_specs=pl.BlockSpec(memory_space=pltpu.VMEM),
        scratch_shapes=[
            pltpu.VMEM((n_cset * rows, channels), bf16),
            pltpu.VMEM((splits, sets), jnp.int32),
            pltpu.VMEM((splits, sets), jnp.int32),
            pltpu.VMEM(table, jnp.float32),
            pltpu.VMEM(table, jnp.float32),
            pltpu.VMEM((table[0], width), jnp.float32),
            pltpu.VMEM((table[0], width), jnp.float32),
            pltpu.VMEM((reach, slots, TILE, TILE), bf16),
            pltpu.VMEM((reach, rows, n_cset * rows), bf16),
            pltpu.VMEM((splits, n_cset * rows, width), bf16),
            pltpu.VMEM((splits, channels, width), bf16),
            pltpu.VMEM((splits, channels, width), bf16),
            pltpu.VMEM((n_cset * rows, channels), bf16),
        ]
        + [pltpu.VMEM((n_cset * rows, channels), bf16)] * (2 * half + 1)
        + [
            dma((4,)),
            dma((reach,)),
            dma((half, CHUNKS)),
            dma((half + 1, n_cset, CHUNKS)),
            dma((half, n_cset, CHUNKS)),
            dma((half + 1, n_cset, CHUNKS)),
            dma((half, n_cset, CHUNKS)),
            dma((n_cset, CHUNKS)),
            dma((n_cset,)),
            dma((n_cset,)),
            dma((n_cset,)),
            dma((n_cset,)),
        ],
        compiler_params=pltpu.CompilerParams(
            collective_id=0, has_side_effects=True, vmem_limit_bytes=56 * 1024 * 1024
        ),
    )(
        jnp.transpose(tile_dst, (0, 2, 1, 3)),
        jnp.transpose(tile_src, (0, 2, 1, 3)),
        tile_count,
        active_table,
        passive_table,
        tiles,
        split_active,
        split_passive,
    )


def solution(mesh):
    in_specs = (
        P(("blk", "cset"), None),
        P(("blk", "cset"), None),
        P("blk", "cset", None, None, None, None),
        P("blk", "cset", None, None),
        P("blk", "cset", None, None),
        P("blk", "cset", None),
        P(),
        P(),
    )
    out_specs = P("blk", "cset")
    return jax.shard_map(local, mesh=mesh, in_specs=in_specs, out_specs=out_specs, check_vma=False)
```

```python
import functools

import jax
import jax.numpy as jnp
from jax import lax
from jax.experimental import pallas as pl
from jax.experimental.pallas import tpu as pltpu
from jax.sharding import PartitionSpec as P

OUTPAD = 1024
TILE = 128
CHUNKS = 4
GROUP = 10
BAND = 128
MESH = pl.DeviceIdType.MESH


def kernel(
    n_blk,
    n_cset,
    half,
    dst_s,
    src_s,
    count_s,
    active_h,
    passive_h,
    adjacency_h,
    left_h,
    right_h,
    out_ref,
    active_v,
    left_raw,
    right_raw,
    left_v,
    right_v,
    left_own,
    right_own,
    tiles_v,
    dense_v,
    active_t,
    sum_t,
    joined_t,
    picked_v,
    choose_left_v,
    choose_right_v,
    *rest,
):
    home = rest[: half + 1]
    away = (None,) + rest[half + 1 : 2 * half + 1]
    (
        local_sem,
        tile_sem,
        own_send,
        side_send,
        sibling_send,
        home_recv,
        away_recv,
        far_send,
        active_send,
        active_recv,
        sum_send,
        sum_recv,
    ) = rest[2 * half + 1 :]
    b = lax.axis_index("blk")
    c = lax.axis_index("cset")
    rows, channels = active_v.shape
    splits, sets = left_raw.shape
    width = out_ref.shape[1]
    bands = width // BAND
    sign = 2 * (b % 2) - 1
    sibling = (b - sign, c)
    others = [(c + i) % n_cset for i in range(1, n_cset)]
    targets = [None] + [
        ((b + k * (1 - 2 * ((b - k + n_blk) % 2)) + n_blk) % n_blk, c) for k in range(1, half + 1)
    ]
    sources = [None] + [((b + sign * k + n_blk) % n_blk, c) for k in range(1, half + 1)]

    barrier = pltpu.get_barrier_semaphore()
    senders = sources[1:] + [sibling] + [(b, o) for o in others]
    for device in senders:
        pl.semaphore_signal(barrier, inc=1, device_id=device, device_id_type=MESH)

    mine = pl.ds(pl.multiple_of(c * rows, rows), rows)
    copies = [
        pltpu.make_async_copy(left_h, left_raw, local_sem.at[0]),
        pltpu.make_async_copy(right_h, right_raw, local_sem.at[1]),
        pltpu.make_async_copy(active_h, active_v, local_sem.at[2]),
        pltpu.make_async_copy(passive_h, home[0].at[mine, :], local_sem.at[3]),
    ]
    for copy in copies[::-1]:
        copy.start()

    def fetch(r):
        return pltpu.make_async_copy(adjacency_h.at[r], tiles_v.at[r], tile_sem.at[r])

    for r in range(2 * half + 1):
        fetch(r).start()
    pl.semaphore_wait(barrier, len(senders))

    size = rows // CHUNKS

    def part(cset, q=0, length=size):
        return pl.ds(pl.multiple_of(cset * rows + q * size, size), length)

    def send(src, dst, send_sem, recv_sem, device):
        copy = pltpu.make_async_remote_copy(
            src_ref=src,
            dst_ref=dst,
            send_sem=send_sem,
            recv_sem=recv_sem,
            device_id=device,
            device_id_type=MESH,
        )
        copy.start()

    def to_others(k, q):
        block = home[k].at[part(c, q), :]
        for i, other in enumerate(others):
            send(block, block, side_send.at[k, i, q], home_recv.at[k, c, q], (b, other))

    def to_sibling(k, cset, q):
        send(
            home[k].at[part(cset, q), :],
            away[k + 1].at[part(cset, q), :],
            sibling_send.at[k, cset, q],
            away_recv.at[k, cset, q],
            sibling,
        )

    def arrived(ref, cset, q, sem):
        block = ref.at[part(cset, q), :]
        pltpu.make_async_copy(block, block, sem).wait()

    copies[3].wait()
    def begin(q, carry):
        block = home[0].at[part(c, q), :]
        for k in range(half, 0, -1):
            goal = home[k].at[part(c, q), :]
            send(block, goal, own_send.at[k - 1, q], home_recv.at[k, c, q], targets[k])
        to_others(0, q)
        to_sibling(0, c, q)
        return carry

    lax.fori_loop(0, CHUNKS, begin, 0)

    copies[0].wait()
    copies[1].wait()
    left_v[...] = jnp.full(left_v.shape, -1, jnp.float32)
    right_v[...] = jnp.full(right_v.shape, -1, jnp.float32)
    left_v[:splits, :sets] = left_raw[...].astype(jnp.float32)
    right_v[:splits, :sets] = right_raw[...].astype(jnp.float32)
    own_columns = pl.ds(pl.multiple_of(c * width, width), width)
    left_own[...] = jnp.transpose(left_v[:, own_columns])
    right_own[...] = jnp.transpose(right_v[:, own_columns])
    copies[2].wait()
    active_t[c] = jnp.transpose(active_v[...])

    def assemble(r):
        fetch(r).wait()
        for d in range(rows // TILE):
            for e in range(n_cset * rows // TILE):
                total = jnp.zeros((TILE, TILE), jnp.bfloat16)
                for t in range(tiles_v.shape[1]):
                    here = (dst_s[0, r, 0, t] == d) & (src_s[0, r, 0, t] == e) & (count_s[0, 0, r] > t)
                    total = total + jnp.where(here, tiles_v[r, t], jnp.zeros_like(total))
                dense_v[r, d * TILE : (d + 1) * TILE, e * TILE : (e + 1) * TILE] = total

    lane = lax.broadcasted_iota(jnp.int32, (BAND, 128), 1)
    channel = [(lane + at).astype(jnp.bfloat16) for at in range(0, channels, 128)]
    one, zero = jnp.ones((BAND, 128), jnp.bfloat16), jnp.zeros((BAND, 128), jnp.bfloat16)

    def one_hot(table, band, choose):
        for j in range(splits):
            column = table[pl.ds(pl.multiple_of(band * BAND, BAND), BAND), j : j + 1]
            wide = jnp.broadcast_to(column, (BAND, 128)).astype(jnp.bfloat16)
            for n, at in enumerate(channel):
                choose[band, j * BAND : (j + 1) * BAND, n * 128 : (n + 1) * 128] = jnp.where(
                    wide == at, one, zero
                )

    def pick(band, cset):
        for g in range(0, splits, GROUP):
            inside = slice(g * BAND, (g + GROUP) * BAND)
            picked = jnp.dot(
                choose_left_v[band, inside, :], active_t[cset], preferred_element_type=jnp.float32
            )
            picked_v[cset, band, inside, :] = picked.astype(jnp.bfloat16)

    def pick_own(band):
        one_hot(left_own, band, choose_left_v)
        one_hot(right_own, band, choose_right_v)
        pick(band, c)

    def pick_others(band):
        for other in others:
            pick(band, other)

    def side_arrived(k, q):
        for other in others:
            arrived(home[k], other, q, home_recv.at[k, other, q])
            if k == 0:
                send(
                    home[0].at[part(other, q), :],
                    home[half].at[part(other, q), :],
                    far_send.at[other, q],
                    home_recv.at[half, other, q],
                    targets[half],
                )
            if k < half:
                to_sibling(k, other, q)

    def own_arrived(k, q):
        arrived(home[k], c, q, home_recv.at[k, c, q])
        if k < half:
            to_others(k, q)
            to_sibling(k, c, q)

    reach = 2 * half + 1

    def advance(g, carry):
        pl.when(g < bands)(functools.partial(pick_own, g))

        @pl.when((g >= 1) & (g <= CHUNKS))
        def _():
            side_arrived(0, g - 1)
            for k in range(1, half + 1):
                own_arrived(k, g - 1)

        @pl.when(g == 1)
        def _():
            for i, other in enumerate(others):
                block = active_t.at[c]
                send(block, block, active_send.at[i], active_recv.at[c], (b, other))

        pl.when(g < reach)(functools.partial(assemble, g))
        return carry

    lax.fori_loop(0, max(bands, reach, CHUNKS + 1), advance, 0)
    for other in others:
        block = active_t.at[other]
        pltpu.make_async_copy(block, block, active_recv.at[other]).wait()

    def forward(g, carry):
        pl.when(g < bands)(functools.partial(pick_others, g))

        @pl.when(g < CHUNKS)
        def _():
            for k in range(1, half):
                side_arrived(k, g)

        return carry

    lax.fori_loop(0, max(bands, CHUNKS), forward, 0)

    def times(r, ref):
        return jnp.dot(dense_v[r], ref[...], preferred_element_type=jnp.float32)

    total = times(half, home[0])
    for k in range(1, half):
        total = total + times(half + sign * k, home[k])
    for k in range(1, half + 1):
        for cset in [c] + others:
            for q in range(CHUNKS):
                arrived(away[k], cset, q, away_recv.at[k - 1, cset, q])
        total = total + times(half - sign * k, away[k])
    for q in range(CHUNKS):
        side_arrived(half, q)
    total = total + times(half + sign * half, home[half])
    sum_t[c] = jnp.transpose(total).astype(jnp.bfloat16)
    for i, other in enumerate(others):
        block = sum_t.at[c]
        send(block, block, sum_send.at[i], sum_recv.at[c], (b, other))

    def join(n, carry):
        i, band = n // bands, n % bands
        owner = (c + i) % n_cset

        @pl.when((i > 0) & (band == 0))
        def _():
            block = sum_t.at[owner]
            pltpu.make_async_copy(block, block, sum_recv.at[owner]).wait()

        total = jnp.zeros((BAND, rows), jnp.float32)
        for g in range(0, splits, GROUP):
            inside = slice(g * BAND, (g + GROUP) * BAND)
            found = jnp.dot(
                choose_right_v[band, inside, :], sum_t[owner], preferred_element_type=jnp.float32
            )
            for j in range(GROUP):
                picked = picked_v[owner, band, (g + j) * BAND : (g + j + 1) * BAND, :]
                total = total + picked.astype(jnp.float32) * found[j * BAND : (j + 1) * BAND, :]
        joined_t[...] = total
        inside = pl.ds(pl.multiple_of(band * BAND, BAND), BAND)
        out_ref[part(owner, 0, rows), inside] = jnp.transpose(joined_t[...]).astype(jnp.bfloat16)
        return carry

    lax.fori_loop(0, n_cset * bands, join, 0)

    def finish(q, carry):
        block = home[0].at[part(c, q), :]
        sems = [own_send.at[k, q] for k in range(half)]
        sems += [side_send.at[k, i, q] for k in range(half) for i in range(n_cset - 1)]
        sems += [sibling_send.at[k, i, q] for k in range(half) for i in range(n_cset)]
        sems += [far_send.at[other, q] for other in others]
        for sem in sems:
            pltpu.make_async_copy(block, block, sem).wait()
        return carry

    lax.fori_loop(0, CHUNKS, finish, 0)
    for i in range(n_cset - 1):
        block = active_t.at[c]
        pltpu.make_async_copy(block, block, active_send.at[i]).wait()
        block = sum_t.at[c]
        pltpu.make_async_copy(block, block, sum_send.at[i]).wait()


def local(
    active_table,
    passive_table,
    adjacency,
    tile_dst,
    tile_src,
    tile_count,
    split_active,
    split_passive,
):
    n_blk, n_cset = lax.axis_size("blk"), lax.axis_size("cset")
    rows, channels = passive_table.shape
    tiles = adjacency[0, 0]
    reach, slots = tiles.shape[:2]
    half = (reach - 1) // 2
    splits, sets = split_active.shape
    width = OUTPAD // n_cset
    hbm = pl.BlockSpec(memory_space=pl.ANY)
    smem = pl.BlockSpec(memory_space=pltpu.SMEM)
    bf16 = jnp.bfloat16
    dma = pltpu.SemaphoreType.DMA
    table = (-(-splits // 128) * 128, OUTPAD)
    return pl.pallas_call(
        functools.partial(kernel, n_blk, n_cset, half),
        out_shape=pltpu.VMEM((n_cset * rows, width), bf16),
        in_specs=[smem] * 3 + [hbm] * 5,
        out_specs=pl.BlockSpec(memory_space=pltpu.VMEM),
        scratch_shapes=[
            pltpu.VMEM((rows, channels), bf16),
            pltpu.VMEM((splits, sets), jnp.int32),
            pltpu.VMEM((splits, sets), jnp.int32),
            pltpu.VMEM(table, jnp.float32),
            pltpu.VMEM(table, jnp.float32),
            pltpu.VMEM((width, table[0]), jnp.float32),
            pltpu.VMEM((width, table[0]), jnp.float32),
            pltpu.VMEM((reach, slots, TILE, TILE), bf16),
            pltpu.VMEM((reach, rows, n_cset * rows), bf16),
            pltpu.VMEM((n_cset, channels, rows), bf16),
            pltpu.VMEM((n_cset, channels, rows), bf16),
            pltpu.VMEM((BAND, rows), jnp.float32),
            pltpu.VMEM((n_cset, width // BAND, splits * BAND, rows), bf16),
            pltpu.VMEM((width // BAND, splits * BAND, channels), bf16),
            pltpu.VMEM((width // BAND, splits * BAND, channels), bf16),
        ]
        + [pltpu.VMEM((n_cset * rows, channels), bf16)] * (2 * half + 1)
        + [
            dma((4,)),
            dma((reach,)),
            dma((half, CHUNKS)),
            dma((half + 1, n_cset, CHUNKS)),
            dma((half, n_cset, CHUNKS)),
            dma((half + 1, n_cset, CHUNKS)),
            dma((half, n_cset, CHUNKS)),
            dma((n_cset, CHUNKS)),
            dma((n_cset,)),
            dma((n_cset,)),
            dma((n_cset,)),
            dma((n_cset,)),
        ],
        compiler_params=pltpu.CompilerParams(
            collective_id=0, has_side_effects=True, vmem_limit_bytes=56 * 1024 * 1024
        ),
    )(
        jnp.transpose(tile_dst, (0, 2, 1, 3)),
        jnp.transpose(tile_src, (0, 2, 1, 3)),
        tile_count,
        active_table,
        passive_table,
        tiles,
        split_active,
        split_passive,
    )


def solution(mesh):
    in_specs = (
        P(("blk", "cset"), None),
        P(("blk", "cset"), None),
        P("blk", "cset", None, None, None, None),
        P("blk", "cset", None, None),
        P("blk", "cset", None, None),
        P("blk", "cset", None),
        P(),
        P(),
    )
    out_specs = P("blk", "cset")
    return jax.shard_map(local, mesh=mesh, in_specs=in_specs, out_specs=out_specs, check_vma=False)
```

```python
import functools

import jax
import jax.numpy as jnp
from jax import lax
from jax.experimental import pallas as pl
from jax.experimental.pallas import tpu as pltpu
from jax.sharding import PartitionSpec as P

OUTPAD = 1024
TILE = 128
CHUNKS = 2
GROUP = 4
MESH = pl.DeviceIdType.MESH


def kernel(
    n_blk,
    n_cset,
    half,
    dst_s,
    src_s,
    count_s,
    active_h,
    passive_h,
    adjacency_h,
    left_h,
    right_h,
    out_ref,
    active_v,
    left_raw,
    right_raw,
    left_v,
    right_v,
    left_own,
    right_own,
    tiles_v,
    dense_v,
    picked_v,
    choose_left_v,
    choose_right_v,
    neighbour_v,
    *rest,
):
    home = rest[: half + 1]
    away = (None,) + rest[half + 1 : 2 * half + 1]
    (
        local_sem,
        tile_sem,
        own_send,
        side_send,
        sibling_send,
        home_recv,
        away_recv,
        far_send,
        active_send,
        active_recv,
        sum_send,
        sum_recv,
    ) = rest[2 * half + 1 :]
    b = lax.axis_index("blk")
    c = lax.axis_index("cset")
    channels = active_v.shape[1]
    rows = active_v.shape[0] // n_cset
    splits, sets = left_raw.shape
    width = out_ref.shape[1]
    piece = min(width, 256)
    sign = 2 * (b % 2) - 1
    sibling = (b - sign, c)
    others = [(c + i) % n_cset for i in range(1, n_cset)]
    targets = [None] + [
        ((b + k * (1 - 2 * ((b - k + n_blk) % 2)) + n_blk) % n_blk, c) for k in range(1, half + 1)
    ]
    sources = [None] + [((b + sign * k + n_blk) % n_blk, c) for k in range(1, half + 1)]

    barrier = pltpu.get_barrier_semaphore()
    senders = sources[1:] + [sibling] + [(b, o) for o in others]
    for device in senders:
        pl.semaphore_signal(barrier, inc=1, device_id=device, device_id_type=MESH)

    mine = pl.ds(pl.multiple_of(c * rows, rows), rows)
    copies = [
        pltpu.make_async_copy(left_h, left_raw, local_sem.at[0]),
        pltpu.make_async_copy(right_h, right_raw, local_sem.at[1]),
        pltpu.make_async_copy(active_h, active_v.at[mine, :], local_sem.at[2]),
        pltpu.make_async_copy(passive_h, home[0].at[mine, :], local_sem.at[3]),
    ]
    for copy in copies[::-1]:
        copy.start()

    def fetch(r):
        return pltpu.make_async_copy(adjacency_h.at[r], tiles_v.at[r], tile_sem.at[r])

    for r in range(2 * half + 1):
        fetch(r).start()
    pl.semaphore_wait(barrier, len(senders))

    size = rows // CHUNKS

    def part(cset, q=0, length=size):
        return pl.ds(pl.multiple_of(cset * rows + q * size, size), length)

    def send(src, dst, send_sem, recv_sem, device):
        copy = pltpu.make_async_remote_copy(
            src_ref=src,
            dst_ref=dst,
            send_sem=send_sem,
            recv_sem=recv_sem,
            device_id=device,
            device_id_type=MESH,
        )
        copy.start()

    def to_others(k, q):
        block = home[k].at[part(c, q), :]
        for i, other in enumerate(others):
            send(block, block, side_send.at[k, i, q], home_recv.at[k, c, q], (b, other))

    def to_sibling(k, cset, q):
        send(
            home[k].at[part(cset, q), :],
            away[k + 1].at[part(cset, q), :],
            sibling_send.at[k, cset, q],
            away_recv.at[k, cset, q],
            sibling,
        )

    def arrived(ref, cset, q, sem):
        block = ref.at[part(cset, q), :]
        pltpu.make_async_copy(block, block, sem).wait()

    copies[3].wait()
    def begin(q, carry):
        block = home[0].at[part(c, q), :]
        for k in range(half, 0, -1):
            goal = home[k].at[part(c, q), :]
            send(block, goal, own_send.at[k - 1, q], home_recv.at[k, c, q], targets[k])
        to_others(0, q)
        to_sibling(0, c, q)
        return carry

    lax.fori_loop(0, CHUNKS, begin, 0)

    copies[0].wait()
    copies[1].wait()
    left_v[...] = jnp.full(left_v.shape, -1, jnp.float32)
    right_v[...] = jnp.full(right_v.shape, -1, jnp.float32)
    left_v[:splits, :sets] = left_raw[...].astype(jnp.float32)
    right_v[:splits, :sets] = right_raw[...].astype(jnp.float32)
    own_columns = pl.ds(pl.multiple_of(c * width, width), width)
    left_own[...] = left_v[:, own_columns]
    right_own[...] = right_v[:, own_columns]
    copies[2].wait()

    def assemble(r):
        fetch(r).wait()
        for d in range(rows // TILE):
            for e in range(n_cset * rows // TILE):
                total = jnp.zeros((TILE, TILE), jnp.bfloat16)
                for t in range(tiles_v.shape[1]):
                    here = (dst_s[0, r, 0, t] == d) & (src_s[0, r, 0, t] == e) & (count_s[0, 0, r] > t)
                    total = total + jnp.where(here, tiles_v[r, t], jnp.zeros_like(total))
                dense_v[r, d * TILE : (d + 1) * TILE, e * TILE : (e + 1) * TILE] = total

    channel = lax.broadcasted_iota(jnp.int32, (channels, piece), 0).astype(jnp.bfloat16)
    one, zero = jnp.ones(channel.shape, jnp.bfloat16), jnp.zeros(channel.shape, jnp.bfloat16)

    def one_hot(table, j, columns):
        row = jnp.broadcast_to(table[pl.ds(j, 1), columns], (16, piece)).astype(jnp.bfloat16)
        return jnp.where(jnp.concatenate([row] * (channels // 16), axis=0) == channel, one, zero)

    def pick(start):
        for j in range(GROUP):
            for at in range(0, width, piece):
                inside = slice(at, at + piece)
                left = one_hot(left_own, start + j, inside)
                choose_left_v[start + j, :, inside] = left
                choose_right_v[start + j, :, inside] = one_hot(right_own, start + j, inside)
                picked = jnp.dot(active_v[mine, :], left, preferred_element_type=jnp.float32)
                picked_v[start + j, mine, inside] = picked.astype(jnp.bfloat16)

    def pick_others(start):
        for other in others:
            there = part(other, 0, rows)
            for j in range(GROUP):
                for at in range(0, width, piece):
                    inside = slice(at, at + piece)
                    picked = jnp.dot(
                        active_v[there, :],
                        choose_left_v[start + j, :, inside],
                        preferred_element_type=jnp.float32,
                    )
                    picked_v[start + j, there, inside] = picked.astype(jnp.bfloat16)

    def side_arrived(k, q):
        for other in others:
            arrived(home[k], other, q, home_recv.at[k, other, q])
            if k == 0:
                send(
                    home[0].at[part(other, q), :],
                    home[half].at[part(other, q), :],
                    far_send.at[other, q],
                    home_recv.at[half, other, q],
                    targets[half],
                )
            if k < half:
                to_sibling(k, other, q)

    def own_arrived(k, q):
        arrived(home[k], c, q, home_recv.at[k, c, q])
        if k < half:
            to_others(k, q)
            to_sibling(k, c, q)

    groups = splits // GROUP
    reach = 2 * half + 1

    def advance(g, carry):
        pl.when(g < groups)(functools.partial(pick, g * GROUP))

        @pl.when((g >= 1) & (g <= CHUNKS))
        def _():
            side_arrived(0, g - 1)
            for k in range(1, half + 1):
                own_arrived(k, g - 1)

        @pl.when(g == 1)
        def _():
            for i, other in enumerate(others):
                block = active_v.at[mine, :]
                send(block, block, active_send.at[i], active_recv.at[c], (b, other))

        pl.when(g < reach)(functools.partial(assemble, g))
        return carry

    lax.fori_loop(0, max(groups, reach, CHUNKS + 1), advance, 0)
    for other in others:
        block = active_v.at[part(other, 0, rows), :]
        pltpu.make_async_copy(block, block, active_recv.at[other]).wait()

    def forward(g, carry):
        pl.when(g < groups)(functools.partial(pick_others, g * GROUP))

        @pl.when(g < CHUNKS)
        def _():
            for k in range(1, half):
                side_arrived(k, g)

        return carry

    lax.fori_loop(0, max(groups, CHUNKS), forward, 0)

    def times(r, ref):
        return jnp.dot(dense_v[r], ref[...], preferred_element_type=jnp.float32)

    total = times(half, home[0])
    for k in range(1, half):
        total = total + times(half + sign * k, home[k])
    for k in range(1, half + 1):
        for cset in [c] + others:
            for q in range(CHUNKS):
                arrived(away[k], cset, q, away_recv.at[k - 1, cset, q])
        total = total + times(half - sign * k, away[k])
    for q in range(CHUNKS):
        side_arrived(half, q)
    total = total + times(half + sign * half, home[half])
    neighbour_v[mine, :] = total.astype(jnp.bfloat16)
    for i, other in enumerate(others):
        block = neighbour_v.at[mine, :]
        send(block, block, sum_send.at[i], sum_recv.at[c], (b, other))
    pieces = width // piece

    def join(n, carry):
        i, p = n // pieces, n % pieces
        owner = (c + i) % n_cset
        there = part(owner, 0, rows)
        inside = pl.ds(pl.multiple_of(p * piece, piece), piece)

        @pl.when((i > 0) & (p == 0))
        def _():
            block = neighbour_v.at[there, :]
            pltpu.make_async_copy(block, block, sum_recv.at[owner]).wait()

        total = jnp.zeros((rows, piece), jnp.float32)
        for j in range(splits):
            found = jnp.dot(
                neighbour_v[there, :],
                choose_right_v[j, :, inside],
                preferred_element_type=jnp.float32,
            )
            total = total + picked_v[j, there, inside].astype(jnp.float32) * found
        out_ref[there, inside] = total.astype(jnp.bfloat16)
        return carry

    lax.fori_loop(0, n_cset * pieces, join, 0)

    def finish(q, carry):
        block = home[0].at[part(c, q), :]
        sems = [own_send.at[k, q] for k in range(half)]
        sems += [side_send.at[k, i, q] for k in range(half) for i in range(n_cset - 1)]
        sems += [sibling_send.at[k, i, q] for k in range(half) for i in range(n_cset)]
        sems += [far_send.at[other, q] for other in others]
        for sem in sems:
            pltpu.make_async_copy(block, block, sem).wait()
        return carry

    lax.fori_loop(0, CHUNKS, finish, 0)
    for i in range(n_cset - 1):
        block = active_v.at[mine, :]
        pltpu.make_async_copy(block, block, active_send.at[i]).wait()
        block = neighbour_v.at[mine, :]
        pltpu.make_async_copy(block, block, sum_send.at[i]).wait()


def local(
    active_table,
    passive_table,
    adjacency,
    tile_dst,
    tile_src,
    tile_count,
    split_active,
    split_passive,
):
    n_blk, n_cset = lax.axis_size("blk"), lax.axis_size("cset")
    rows, channels = passive_table.shape
    tiles = adjacency[0, 0]
    reach, slots = tiles.shape[:2]
    half = (reach - 1) // 2
    splits, sets = split_active.shape
    width = OUTPAD // n_cset
    hbm = pl.BlockSpec(memory_space=pl.ANY)
    smem = pl.BlockSpec(memory_space=pltpu.SMEM)
    bf16 = jnp.bfloat16
    dma = pltpu.SemaphoreType.DMA
    table = (-(-splits // 8) * 8, OUTPAD)
    return pl.pallas_call(
        functools.partial(kernel, n_blk, n_cset, half),
        out_shape=pltpu.VMEM((n_cset * rows, width), bf16),
        in_specs=[smem] * 3 + [hbm] * 5,
        out_specs=pl.BlockSpec(memory_space=pltpu.VMEM),
        scratch_shapes=[
            pltpu.VMEM((n_cset * rows, channels), bf16),
            pltpu.VMEM((splits, sets), jnp.int32),
            pltpu.VMEM((splits, sets), jnp.int32),
            pltpu.VMEM(table, jnp.float32),
            pltpu.VMEM(table, jnp.float32),
            pltpu.VMEM((table[0], width), jnp.float32),
            pltpu.VMEM((table[0], width), jnp.float32),
            pltpu.VMEM((reach, slots, TILE, TILE), bf16),
            pltpu.VMEM((reach, rows, n_cset * rows), bf16),
            pltpu.VMEM((splits, n_cset * rows, width), bf16),
            pltpu.VMEM((splits, channels, width), bf16),
            pltpu.VMEM((splits, channels, width), bf16),
            pltpu.VMEM((n_cset * rows, channels), bf16),
        ]
        + [pltpu.VMEM((n_cset * rows, channels), bf16)] * (2 * half + 1)
        + [
            dma((4,)),
            dma((reach,)),
            dma((half, CHUNKS)),
            dma((half + 1, n_cset, CHUNKS)),
            dma((half, n_cset, CHUNKS)),
            dma((half + 1, n_cset, CHUNKS)),
            dma((half, n_cset, CHUNKS)),
            dma((n_cset, CHUNKS)),
            dma((n_cset,)),
            dma((n_cset,)),
            dma((n_cset,)),
            dma((n_cset,)),
        ],
        compiler_params=pltpu.CompilerParams(
            collective_id=0, has_side_effects=True, vmem_limit_bytes=56 * 1024 * 1024
        ),
    )(
        jnp.transpose(tile_dst, (0, 2, 1, 3)),
        jnp.transpose(tile_src, (0, 2, 1, 3)),
        tile_count,
        active_table,
        passive_table,
        tiles,
        split_active,
        split_passive,
    )


def solution(mesh):
    in_specs = (
        P(("blk", "cset"), None),
        P(("blk", "cset"), None),
        P("blk", "cset", None, None, None, None),
        P("blk", "cset", None, None),
        P("blk", "cset", None, None),
        P("blk", "cset", None),
        P(),
        P(),
    )
    out_specs = P("blk", "cset")
    return jax.shard_map(local, mesh=mesh, in_specs=in_specs, out_specs=out_specs, check_vma=False)
```
